512 devices in a mesh: seq: 128 (over y, z, core), head: 4 (over x).
Axes of the slice: x: 4, y: 4, z: 16, core: 2. Of those that a mesh axis runs over, the one named last changes fastest.
Arguments:
- query_rows: bfloat16 [16384, 512], P('seq', 'head'), may hold values from -6 to 6
- key_rows: bfloat16 [16384, 512], P('seq', 'head'), may hold values from -6 to 6
- value_rows: bfloat16 [16384, 512], P('seq', 'head'), may hold values from -6 to 6
- gate_rows: bfloat16 [16384, 512], P('seq', 'head'), may hold values from -6 to 6
- cotangent: bfloat16 [16384, 512], P('seq', 'head'), may hold values from -6 to 6
- event_gaps: int32 [16384], P('seq'), may hold values from 0 to 7
- block_lists: int32 [128, 8], replicated, may hold values from -1 to 126, as said below
- bias_table: float32 [8, 16], P('head'), may hold values from -1 to 1
- norm_gain: float32 [512], P('head'), may hold values from 0.1 to 1.9
Outputs:
- layer_out: bfloat16 [16384, 512], P('seq', 'head')
- grad_query: bfloat16 [16384, 512], P('seq', 'head')
- grad_key: bfloat16 [16384, 512], P('seq', 'head')
- grad_value: bfloat16 [16384, 512], P('seq', 'head')
- grad_gate: bfloat16 [16384, 512], P('seq', 'head')
The draws below stay inside these ranges and needn't reach their ends.
Inputs may be any that keep to these rules, and one draw needn't show every extreme that they name: `block_lists`: slot s of row c holds either c - 2**s or -1; it holds -1 wherever 2**s >= 128 or 2**s > c. The last row lists every group c - 2**s that exists.
All inputs are finite; a program needn't handle non-finite values.
Results may differ from the reference program's by a relative error of at most 0.01.
Values may be sent and summed in bfloat16 or wider, within the bound.
No kernel may reach another device: no remote copies, remote signals or barrier semaphores. Data moves between devices by JAX's collectives and lax.ppermute only.
A program may use at most 64 MiB of HBM per device.

```python
import jax
import jax.numpy as jnp
from jax import lax

H = 8
DH = 64
D = 512
C = 128
NB = 8
NBK = 16
NCH = 128
L = 16384


def draw_block_lists(key, part):
    group_ids = jnp.arange(NCH, dtype=jnp.int32)[:, None]
    slot_ids = jnp.arange(NB, dtype=jnp.int32)[None, :]
    distance = jnp.left_shift(jnp.int32(1), slot_ids)
    density = jax.random.randint(jax.random.fold_in(key, 11), (NCH, 1), 1, 5)
    coins = jax.random.randint(jax.random.fold_in(key, 12), (NCH, NB), 0, 4)
    exists = (distance < NCH) & (group_ids - distance >= 0)
    chosen = (coins < density) | (group_ids == NCH - 1)
    return jnp.where(exists & chosen, group_ids - distance, -1).astype(jnp.int32)


def plant(entries, rng, least, high):
    dims = entries.shape
    place = [jax.random.randint(jax.random.fold_in(rng, axis), (), 0, dims[axis]) for axis in range(len(dims))]
    entries = entries.at[tuple(place)].set(least)
    longest = dims.index(max(dims))
    place[longest] = (place[longest] + 1) % dims[longest]
    return entries.at[tuple(place)].set(high)


def level_of(own_key, extent, pieces, low, largest):
    def one(dim, shards_of):
        heights = jax.random.uniform(jax.random.fold_in(jax.random.fold_in(own_key, 6), dim), (shards_of,), jnp.float32, low / len(pieces), largest / len(pieces))
        return jnp.repeat(jnp.exp(heights), extent[dim] // shards_of).reshape((-1,) + (1,) * (len(extent) - dim - 1))

    loudness = one(*pieces[0])
    for cut in pieces[1:]:
        loudness = loudness * one(*cut)
    return loudness


def bell_draw(stream_key, extent, spread, most, pieces=(), kind=jnp.bfloat16):
    level = level_of(stream_key, extent, pieces, -0.22, 0.18) if pieces else 1.0
    values = jax.random.normal(stream_key, extent, jnp.float32) * spread * level
    return jnp.minimum(jnp.maximum(values, -most), most).astype(kind)


def setup_inputs(seed: int = 0) -> dict:
    splits = jax.random.split(jax.random.key(seed), 10)
    return {
        "query_rows": bell_draw(splits[0], (L, D), 1.0, 6.0, ((0, 128), (1, 4))),
        "key_rows": bell_draw(splits[1], (L, D), 1.0, 6.0, ((0, 128), (1, 4))),
        "value_rows": bell_draw(splits[2], (L, D), 1.0, 6.0, ((0, 128), (1, 4))),
        "gate_rows": bell_draw(splits[3], (L, D), 1.0, 6.0, ((0, 128), (1, 4))),
        "cotangent": bell_draw(splits[4], (L, D), 1.0, 6.0, ((0, 128), (1, 4))),
        "event_gaps": plant(jax.random.randint(splits[5], (L,), 0, 8), jax.random.fold_in(splits[5], 1), 0, 7).astype(jnp.int32),
        "block_lists": draw_block_lists(jax.random.fold_in(splits[9], 71), 0),
        "bias_table": jnp.clip(jax.random.uniform(splits[7], (H, NBK), jnp.float32, -1.0, 1.0) * level_of(splits[7], (H, NBK), ((0, 4),), -0.4, 0.0), -1.0, 1.0),
        "norm_gain": jnp.clip(1.0 + 0.18 * jax.random.normal(splits[8], (D,), jnp.float32), 0.1, 1.9),
    }


norm_eps = 1e-05

def bucket_bias(delta, table):
    bias = jnp.zeros((table.shape[0],) + delta.shape, jnp.float32) + table[:, 0][:, None, None]
    for bucket_id in range(1, table.shape[1]):
        increment = (table[:, bucket_id] - table[:, bucket_id - 1])[:, None, None]
        reached = (delta >= 2 ** (bucket_id - 1)).astype(jnp.float32)
        bias = bias + increment * reached[None]
    return bias

def causal_mask(length):
    later_ids = lax.broadcasted_iota(jnp.int32, (length, length), 1)
    early_ids = lax.broadcasted_iota(jnp.int32, (length, length), 0)
    return (later_ids <= early_ids).astype(jnp.float32)

def block_scores(query_heads, key_heads, query_times, key_times, table, scaling):
    scores = jnp.einsum('qhd,khd->hqk', query_heads.astype(jnp.float32), key_heads.astype(jnp.float32)) * scaling
    return scores + bucket_bias(query_times[:, None] - key_times[None, :], table)

def pick_group(array, index):
    return lax.dynamic_index_in_dim(array, index, 0, keepdims=False)

def reference(query_rows, key_rows, value_rows, gate_rows, cotangent, event_gaps, block_lists, bias_table, norm_gain):
    scaling = DH ** (-0.5)
    event_times = jnp.cumsum(event_gaps).astype(jnp.int32)
    query_all = query_rows.reshape(NCH, C, H, DH)
    key_all = key_rows.reshape(NCH, C, H, DH)
    value_all = value_rows.reshape(NCH, C, H, DH)
    gate_all = gate_rows.reshape(NCH, C, D)
    upstream_all = cotangent.reshape(NCH, C, D)
    times_all = event_times.reshape(NCH, C)
    diagonal = causal_mask(C)
    offsets = [(slot_id, 2 ** slot_id) for slot_id in range(NB) if 2 ** slot_id < NCH]

    def one_group(accum, group_id):
        key_grad, value_grad = accum
        query_heads = pick_group(query_all, group_id)
        query_times = pick_group(times_all, group_id)
        sources = [(group_id, group_id >= 0, True)]
        for slot_id, distance in offsets:
            sources.append((jnp.maximum(group_id - distance, 0), block_lists[group_id, slot_id] >= 0, False))
        attended = jnp.zeros((C, H, DH), jnp.float32)
        for source, listed, on_diag in sources:
            key_heads = pick_group(key_all, source)
            value_heads = pick_group(value_all, source)
            scores = block_scores(query_heads, key_heads, query_times, pick_group(times_all, source), bias_table, scaling)
            weights = jax.nn.silu(scores)
            if on_diag:
                weights = weights * diagonal[None]
            weights = weights.astype(jnp.bfloat16)
            added = jnp.einsum('hqk,khd->qhd', weights.astype(jnp.float32), value_heads.astype(jnp.float32))
            attended = attended + jnp.where(listed, added, 0.0)
        flat = attended.reshape(C, D)
        row_mean = lax.optimization_barrier(jnp.sum(flat, axis=1)) / D
        row_var = lax.optimization_barrier(jnp.sum(flat * flat, axis=1)) / D - row_mean * row_mean
        inv_std = lax.rsqrt(row_var + norm_eps)
        centered = (flat - row_mean[:, None]) * inv_std[:, None]
        normed = centered * norm_gain[None, :]
        gates = pick_group(gate_all, group_id).astype(jnp.float32)
        upstream = pick_group(upstream_all, group_id).astype(jnp.float32)
        layer_out = (normed * gates).astype(jnp.bfloat16)
        grad_gate = (upstream * normed).astype(jnp.bfloat16)
        scaled = upstream * gates * norm_gain[None, :]
        grad_attended = inv_std[:, None] * (scaled - lax.optimization_barrier(jnp.sum(scaled, axis=1))[:, None] / D - centered * lax.optimization_barrier(jnp.sum(scaled * centered, axis=1))[:, None] / D)
        grad_heads = grad_attended.astype(jnp.bfloat16).reshape(C, H, DH)
        grad_query = jnp.zeros((C, H, DH), jnp.float32)
        for source, listed, on_diag in sources:
            key_heads = pick_group(key_all, source)
            value_heads = pick_group(value_all, source)
            scores = block_scores(query_heads, key_heads, query_times, pick_group(times_all, source), bias_table, scaling)
            sigmoid_val = jax.nn.sigmoid(scores)
            weights = jax.nn.silu(scores)
            slope = sigmoid_val * (1.0 + scores * (1.0 - sigmoid_val))
            grad_weights = jnp.einsum('qhd,khd->hqk', grad_heads.astype(jnp.float32), value_heads.astype(jnp.float32))
            grad_scores = grad_weights * slope
            if on_diag:
                weights = weights * diagonal[None]
                grad_scores = grad_scores * diagonal[None]
            weights = weights.astype(jnp.bfloat16).astype(jnp.float32)
            grad_scores = grad_scores.astype(jnp.bfloat16).astype(jnp.float32)
            query_part = jnp.einsum('hqk,khd->qhd', grad_scores, key_heads.astype(jnp.float32)) * scaling
            key_part = jnp.einsum('hqk,qhd->khd', grad_scores, query_heads.astype(jnp.float32)) * scaling
            value_part = jnp.einsum('hqk,qhd->khd', weights, grad_heads.astype(jnp.float32))
            grad_query = grad_query + jnp.where(listed, query_part, 0.0)
            key_grad = key_grad.at[source].add(jnp.where(listed, key_part, 0.0))
            value_grad = value_grad.at[source].add(jnp.where(listed, value_part, 0.0))
        return ((key_grad, value_grad), (layer_out, grad_query.reshape(C, D).astype(jnp.bfloat16), grad_gate))
    start = (jnp.zeros((NCH, C, H, DH), jnp.float32), jnp.zeros((NCH, C, H, DH), jnp.float32))
    finals, stacked = lax.scan(one_group, start, jnp.arange(NCH, dtype=jnp.int32))
    layer_out = stacked[0].reshape(L, D)
    grad_query = stacked[1].reshape(L, D)
    grad_gate = stacked[2].reshape(L, D)
    grad_key = finals[0].reshape(L, D).astype(jnp.bfloat16)
    grad_value = finals[1].reshape(L, D).astype(jnp.bfloat16)
    return (layer_out, grad_query, grad_key, grad_value, grad_gate)
```

```python
import jax
import jax.numpy as jnp
from jax import lax
from jax.experimental import pallas as pl
from jax.experimental.pallas import tpu as pltpu
from jax.sharding import PartitionSpec as P

norm_eps = 1e-05
C = 128
F = 128
DH = 64
DISTANCES = (1, 2, 4, 8, 16, 32, 64)
ROW = 32
PAD = 16
WIDE = 512.0
f32, bf16, i32 = jnp.float32, jnp.bfloat16, jnp.int32
VMEM = pl.BlockSpec(memory_space=pltpu.VMEM)
PARAMS = pltpu.CompilerParams(vmem_limit_bytes=40 * 1024 * 1024)


def iota(shape, dim):
    return lax.broadcasted_iota(i32, shape, dim)


def by_head(rows):
    left = iota(rows.shape, 1) < DH
    zero = jnp.zeros_like(rows)
    return jnp.concatenate([jnp.where(left, rows, zero), jnp.where(left, zero, rows)], axis=0)


def from_heads(both):
    left = iota((C, F), 1) < DH
    return jnp.where(left, both[:C], both[C:])


def dot(a, b, dims, precision=None):
    return lax.dot_general(a, b, (dims, ((), ())), preferred_element_type=f32, precision=precision)


NN, NT, TN = ((1,), (0,)), ((1,), (1,)), ((0,), (0,))


def pack_kernel(key_ref, value_ref, gaps_ref, out_ref):
    out_ref[:C, :F] = key_ref[...]
    out_ref[:C, F:] = value_ref[...]
    gaps = jnp.broadcast_to(gaps_ref[...].astype(f32), (PAD, C))
    out_ref[C:, :F] = gaps.astype(bf16)
    out_ref[C:, F:] = gaps.astype(bf16)


def forward_kernel(
    group_ref,
    query_ref,
    gate_ref,
    cot_ref,
    gain_ref,
    lists_ref,
    table_ref,
    totals_ref,
    *refs,
):
    packets, (att_ref, sums_ref, weights_ref, slopes_ref) = refs[:8], refs[8:]
    group = group_ref[0]
    place = lax.rem(group, ROW)
    queries = by_head((query_ref[...].astype(f32) * 0.125).astype(bf16))
    gaps = jnp.concatenate([p[C : C + 1, :F] for p in packets], axis=0)
    upper = (iota((C, C), 0) <= iota((C, C), 1)).astype(bf16)
    key_times = dot(gaps, upper, NN)
    lower = (iota((C, C), 1) <= iota((C, C), 0)).astype(bf16)
    query_times = dot(lower, gaps, NT)[:, :1]
    totals = totals_ref[...].reshape(ROW, C)
    back = place - iota((ROW, C), 0) + ROW * iota((ROW, C), 1)
    sums = [jnp.zeros((1, C), f32)]
    for distance in DISTANCES:
        inside = (back >= 1) & (back <= distance)
        sums.append(jnp.sum(jnp.where(inside, totals, 0.0), axis=0, keepdims=True))
    between = jnp.sum(jnp.concatenate(sums, axis=0), axis=1, keepdims=True)
    shifts = between - key_times
    listed = lists_ref[pl.ds(group, 1), :]
    tables = [jnp.broadcast_to(jnp.pad(table_ref[h : h + 1, :], ((0, 0), (0, C - 16))), (C, C)) for h in range(2)]
    acc = jnp.zeros((2 * C, F), f32)
    for b, packet in enumerate(packets):
        scores = dot(queries, packet[:C, :F], NT)
        delta = (query_times + shifts[b : b + 1, :]).astype(i32)
        bucket = jnp.minimum(32 - lax.clz(delta), 15)
        bias = jnp.concatenate([jnp.take_along_axis(t, bucket, axis=1) for t in tables], axis=0)
        scores = scores + bias
        sig = 0.5 * jnp.tanh(0.5 * scores) + 0.5
        silu = scores * sig
        slope = sig + silu * (1.0 - sig)
        if b == 0:
            keep = (iota((C, C), 1) <= iota((C, C), 0)).astype(f32)
            keep = jnp.concatenate([keep, keep], axis=0)
        else:
            keep = (listed[:, b - 1 : b] >= 0).astype(f32)
        weights = (silu * keep).astype(bf16)
        weights_ref[:, b * C : (b + 1) * C] = weights
        slopes_ref[:, b * C : (b + 1) * C] = slope * keep
        acc = acc + dot(weights, packet[:C, F:], NN)
    att = from_heads(acc)
    att_ref[...] = att
    scaled = cot_ref[...].astype(f32) * gate_ref[...].astype(f32) * gain_ref[...]
    terms = jnp.concatenate([att, att * att, scaled, scaled * att], axis=0)
    rows = dot(jnp.ones((8, F), f32), terms, NT, lax.Precision.HIGHEST)
    for r in range(4):
        sums_ref[r : r + 1, :] = rows[0:1, r * C : (r + 1) * C]


def backward_kernel(
    query_ref,
    gate_ref,
    cot_ref,
    gain_ref,
    att_ref,
    sums_ref,
    weights_ref,
    slopes_ref,
    *refs,
):
    packets, (out_ref, dq_ref, dgate_ref, own_ref), sent = refs[:8], refs[8:12], refs[12:]
    sums = jnp.concatenate([sums_ref[...], jnp.zeros((4, C), f32)], axis=0)
    cols = jnp.transpose(sums) * (1.0 / WIDE)
    mean, square, mean_scaled, mean_cross = (cols[:, r : r + 1] for r in range(4))
    inv_std = lax.rsqrt(square - mean * mean + norm_eps)
    mean_cross = (mean_cross - mean * mean_scaled) * inv_std
    centered = (att_ref[...] - mean) * inv_std
    gain, gates, cot = gain_ref[...], gate_ref[...].astype(f32), cot_ref[...].astype(f32)
    normed = centered * gain
    out_ref[...] = (normed * gates).astype(bf16)
    dgate_ref[...] = (cot * normed).astype(bf16)
    scaled = cot * gates * gain
    grads = by_head((inv_std * (scaled - mean_scaled - centered * mean_cross)).astype(bf16))
    queries = by_head((query_ref[...].astype(f32) * 0.125).astype(bf16))
    acc = jnp.zeros((2 * C, F), f32)
    for b, packet in enumerate(packets):
        at = slice(b * C, (b + 1) * C)
        grad_weights = dot(grads, packet[:C, F:], NT)
        grad_scores = (grad_weights * slopes_ref[:, at]).astype(bf16)
        acc = acc + dot(grad_scores, packet[:C, :F], NN)
        dkey = dot(grad_scores, queries, TN)
        dvalue = dot(weights_ref[:, at], grads, TN)
        target = own_ref if b == 0 else sent[b - 1]
        target[:, :F] = dkey.astype(target.dtype)
        target[:, F:] = dvalue.astype(target.dtype)
    dq_ref[...] = (from_heads(acc) * 0.125).astype(bf16)


def total_kernel(own_ref, *refs):
    parts, (dk_ref, dv_ref) = refs[:7], refs[7:]
    total = own_ref[...]
    for part in parts:
        total = total + part[...].astype(f32)
    dk_ref[...] = total[:, :F].astype(bf16)
    dv_ref[...] = total[:, F:].astype(bf16)


def call(kernel, outs, smem=0):
    def run(*args):
        specs = [pl.BlockSpec(memory_space=pltpu.SMEM)] * smem + [VMEM] * (len(args) - smem)
        return pl.pallas_call(
            kernel,
            out_shape=[jax.ShapeDtypeStruct(s, t) for s, t in outs],
            in_specs=specs,
            out_specs=[VMEM] * len(outs),
            compiler_params=PARAMS,
        )(*args)

    return run


def shifted(x, by):
    count = lax.axis_size("seq")
    return lax.ppermute(x, "seq", [(i, i + by) for i in range(count) if 0 <= i + by < count])


def per_device(
    query_rows,
    key_rows,
    value_rows,
    gate_rows,
    cotangent,
    event_gaps,
    block_lists,
    bias_table,
    norm_gain,
):
    count = lax.axis_size("seq")
    group = lax.axis_index("seq").astype(i32).reshape(1)
    gain = norm_gain.reshape(1, F)
    (packet,) = call(pack_kernel, [((C + PAD, 2 * F), bf16)])(
        key_rows, value_rows, event_gaps.reshape(1, C)
    )
    fetched = {d: shifted(packet, d) for d in (64, 32)}
    fetched |= {d: shifted(packet, d) for d in (16, 8, 4, 2, 1)}
    three = [jnp.sum(p[C, :F].astype(f32)) for p in (packet, fetched[32], fetched[64])]
    lanes = lax.iota(i32, C)
    mine = sum(jnp.where(lanes == k, t, 0.0) for k, t in enumerate(three))
    rows = [[y * ROW + k for k in range(ROW)] for y in range(count // ROW)]
    totals = lax.all_to_all(
        jnp.broadcast_to(mine, (ROW, 1, C)), "seq", 0, 0, axis_index_groups=rows
    )
    packets = [packet] + [fetched[d] for d in DISTANCES]
    att, sums, weights, slopes = call(
        forward_kernel,
        [((C, F), f32), ((4, C), f32), ((2 * C, 8 * C), bf16), ((2 * C, 8 * C), f32)],
        1,
    )(
        group,
        query_rows,
        gate_rows,
        cotangent,
        gain,
        block_lists,
        bias_table,
        totals,
        *packets,
    )
    sums = lax.psum(sums, "head")
    layer_out, grad_query, grad_gate, own, *sent = call(
        backward_kernel,
        [((C, F), bf16)] * 3 + [((C, 2 * F), f32)] + [((C, 2 * F), bf16)] * 7,
    )(query_rows, gate_rows, cotangent, gain, att, sums, weights, slopes, *packets)
    order = (4, 3, 2, 1, 0, 6, 5)
    returned = [shifted(sent[s], -DISTANCES[s]) for s in order]
    grad_key, grad_value = call(total_kernel, [((C, F), bf16)] * 2)(own, *returned)
    return layer_out, grad_query, grad_key, grad_value, grad_gate


def solution(mesh):
    rows = P("seq", "head")
    return jax.shard_map(
        per_device,
        mesh=mesh,
        in_specs=(rows, rows, rows, rows, rows, P("seq"), P(), P("head", None), P("head")),
        out_specs=(rows, rows, rows, rows, rows),
        check_vma=False,
    )
```

```python
import functools

import jax
import jax.numpy as jnp
from jax import lax
from jax.experimental import pallas as pl
from jax.experimental.pallas import tpu as pltpu
from jax.sharding import PartitionSpec as P

norm_eps = 1e-05
C = 128
F = 128
DH = 64
DISTANCES = (1, 2, 4, 8, 16, 32, 64)
ROW = 32
PAD = 16
WIDE = 512.0
f32, bf16, i32 = jnp.float32, jnp.bfloat16, jnp.int32
VMEM = pl.BlockSpec(memory_space=pltpu.VMEM)
PARAMS = pltpu.CompilerParams(vmem_limit_bytes=40 * 1024 * 1024)


def iota(shape, dim):
    return lax.broadcasted_iota(i32, shape, dim)


def by_head(rows):
    left = iota(rows.shape, 1) < DH
    zero = jnp.zeros_like(rows)
    return jnp.concatenate([jnp.where(left, rows, zero), jnp.where(left, zero, rows)], axis=0)


def from_heads(both):
    left = iota((C, F), 1) < DH
    return jnp.where(left, both[:C], both[C:])


def dot(a, b, dims, precision=None):
    return lax.dot_general(a, b, (dims, ((), ())), preferred_element_type=f32, precision=precision)


NN, NT, TN = ((1,), (0,)), ((1,), (1,)), ((0,), (0,))


def pack_kernel(key_ref, value_ref, gaps_ref, out_ref, totals_ref, gaps_buf, sems):
    copies = [
        pltpu.make_async_copy(gaps_ref, gaps_buf, sems.at[0]),
        pltpu.make_async_copy(key_ref, out_ref.at[pl.ds(0, C), pl.ds(0, F)], sems.at[1]),
        pltpu.make_async_copy(value_ref, out_ref.at[pl.ds(0, C), pl.ds(F, F)], sems.at[2]),
    ]
    for copy in copies:
        copy.start()
    copies[0].wait()
    gaps = gaps_buf[...].astype(f32)
    total = jnp.sum(gaps, axis=1, keepdims=True)
    totals_ref[...] = jnp.broadcast_to(total.reshape(1, 1, 1), (ROW, 1, C))
    gaps = jnp.broadcast_to(gaps, (PAD, C)).astype(bf16)
    out_ref[C:, :F] = gaps
    out_ref[C:, F:] = gaps
    copies[1].wait()
    copies[2].wait()


def row_kernel(packet_ref, totals_ref, out_ref):
    out_ref[:C, :] = packet_ref[:C, :]
    totals = totals_ref[...].reshape(ROW, C)
    totals = jnp.where(iota((ROW, C), 0) == iota((ROW, C), 1), totals, 0.0)
    totals = jnp.sum(totals, axis=0, keepdims=True)
    high = jnp.floor(totals * 0.0625)
    low = totals - 16.0 * high
    line = iota((PAD, C), 0)
    gaps = packet_ref[C:, :F].astype(f32)
    out_ref[C:, :F] = jnp.where(line == 1, high, jnp.where(line == 2, low, gaps)).astype(bf16)
    out_ref[C:, F:] = packet_ref[C:, F:]


def prepare_kernel(query_ref, gate_ref, cot_ref, gain_ref, table_ref, lists_ref, *outs):
    heads_ref, scaled_ref, table_out_ref, lists_out_ref = outs
    heads_ref[...] = by_head((query_ref[...].astype(f32) * 0.125).astype(bf16))
    scaled_ref[...] = cot_ref[...].astype(f32) * gate_ref[...].astype(f32) * gain_ref[...]
    table_out_ref[...] = jnp.pad(table_ref[...], ((0, 0), (0, C - 16)))
    lists_out_ref[...] = lists_ref[...]


def forward_kernel(group_ref, heads_ref, scaled_ref, lists_ref, table_ref, totals_ref, *refs):
    packets, (att_ref, sums_ref, weights_ref, slopes_ref) = refs[:8], refs[8:]
    group = group_ref[0]
    place = lax.rem(group, ROW)
    queries = heads_ref[...]
    gaps = jnp.concatenate([p[C : C + 1, :F] for p in packets], axis=0)
    upper = (iota((C, C), 0) <= iota((C, C), 1)).astype(bf16)
    key_times = dot(gaps, upper, NN)
    lower = (iota((C, C), 1) <= iota((C, C), 0)).astype(bf16)
    query_times = dot(lower, gaps, NT)[:, :1]
    own = totals_ref[...].reshape(ROW, C)
    own = jnp.where(iota((ROW, C), 0) == iota((ROW, C), 1), own, 0.0)
    totals = [jnp.sum(own, axis=0, keepdims=True)]
    for packet in packets[6:]:
        part = packet[C:, :F].astype(f32)
        totals.append(part[1:2, :] * 16.0 + part[2:3, :])
    lane = iota((8, C), 1)
    distance = jnp.left_shift(1, iota((8, C), 0)) >> 1
    between = jnp.zeros((8, C), f32)
    for r, total in enumerate(totals):
        back = place - lane + ROW * r
        inside = (back >= 1) & (back <= distance) & (lane < ROW)
        between = between + jnp.where(inside, total, 0.0)
    shifts = jnp.sum(between, axis=1, keepdims=True) - key_times
    listed = jnp.where(lane == group, lists_ref[...], 0)
    listed = jnp.sum(listed.astype(f32), axis=1, keepdims=True) >= 0.0
    listed = listed.astype(f32)
    tables = [jnp.broadcast_to(table_ref[h : h + 1, :], (C, C)) for h in range(2)]
    acc = jnp.zeros((2 * C, F), f32)
    for b, packet in enumerate(packets):
        scores = dot(queries, packet[:C, :F], NT)
        delta = (query_times + shifts[b : b + 1, :]).astype(i32)
        bucket = jnp.minimum(32 - lax.clz(delta), 15)
        bias = jnp.concatenate([jnp.take_along_axis(t, bucket, axis=1) for t in tables], axis=0)
        scores = scores + bias
        sig = 0.5 * jnp.tanh(0.5 * scores) + 0.5
        silu = scores * sig
        slope = sig + silu * (1.0 - sig)
        if b == 0:
            keep = (iota((C, C), 1) <= iota((C, C), 0)).astype(f32)
            keep = jnp.concatenate([keep, keep], axis=0)
        else:
            keep = listed[b - 1 : b, :]
        weights = (silu * keep).astype(bf16)
        weights_ref[:, b * C : (b + 1) * C] = weights
        slopes_ref[:, b * C : (b + 1) * C] = slope * keep
        acc = acc + dot(weights, packet[:C, F:], NN)
    att = from_heads(acc)
    att_ref[...] = att
    scaled = scaled_ref[...]
    terms = jnp.concatenate([att, att * att, scaled, scaled * att], axis=0)
    rows = dot(jnp.ones((8, F), f32), terms, NT, lax.Precision.HIGHEST)
    for r in range(4):
        sums_ref[r : r + 1, :] = rows[0:1, r * C : (r + 1) * C]


def norm_terms(sums_ref, att_ref):
    sums = jnp.concatenate([sums_ref[...], jnp.zeros((4, C), f32)], axis=0)
    cols = jnp.transpose(sums) * (1.0 / WIDE)
    mean, square, mean_scaled, mean_cross = (cols[:, r : r + 1] for r in range(4))
    inv_std = lax.rsqrt(square - mean * mean + norm_eps)
    mean_cross = (mean_cross - mean * mean_scaled) * inv_std
    return inv_std, (att_ref[...] - mean) * inv_std, mean_scaled, mean_cross


def block_grads(b, queries, grads, weights_ref, slopes_ref, packet, out_ref):
    at = slice(b * C, (b + 1) * C)
    grad_weights = dot(grads, packet[:C, F:], NT)
    grad_scores = (grad_weights * slopes_ref[:, at]).astype(bf16)
    out_ref[:, :F] = dot(grad_scores, queries, TN).astype(out_ref.dtype)
    out_ref[:, F:] = dot(weights_ref[:, at], grads, TN).astype(out_ref.dtype)
    return dot(grad_scores, packet[:C, :F], NN)


def first_backward(blocks, att_ref, sums_ref, heads_ref, scaled_ref, weights_ref, slopes_ref, *refs):
    n = len(blocks)
    packets, grads_ref, acc_ref, sent = refs[:n], refs[n], refs[n + 1], refs[n + 2 :]
    inv_std, centered, mean_scaled, mean_cross = norm_terms(sums_ref, att_ref)
    grads = inv_std * (scaled_ref[...] - mean_scaled - centered * mean_cross)
    grads = by_head(grads.astype(bf16))
    grads_ref[...] = grads
    queries = heads_ref[...]
    acc = jnp.zeros((2 * C, F), f32)
    for b, packet, out in zip(blocks, packets, sent):
        acc = acc + block_grads(b, queries, grads, weights_ref, slopes_ref, packet, out)
    acc_ref[...] = acc


def next_backward(blocks, grads_ref, before_ref, heads_ref, weights_ref, slopes_ref, *refs):
    n = len(blocks)
    packets, acc_ref, sent = refs[:n], refs[n], refs[n + 1 :]
    grads, queries, acc = grads_ref[...], heads_ref[...], before_ref[...]
    for b, packet, out in zip(blocks, packets, sent):
        acc = acc + block_grads(b, queries, grads, weights_ref, slopes_ref, packet, out)
    acc_ref[...] = acc


def last_backward(
    grads_ref, before_ref, heads_ref, weights_ref, slopes_ref, packet, att_ref, sums_ref, gate_ref, cot_ref, gain_ref, *outs
):
    out_ref, dq_ref, dgate_ref, own_ref = outs
    acc = before_ref[...] + block_grads(
        0, heads_ref[...], grads_ref[...], weights_ref, slopes_ref, packet, own_ref
    )
    dq_ref[...] = (from_heads(acc) * 0.125).astype(bf16)
    centered = norm_terms(sums_ref, att_ref)[1]
    normed = centered * gain_ref[...]
    out_ref[...] = (normed * gate_ref[...].astype(f32)).astype(bf16)
    dgate_ref[...] = (cot_ref[...].astype(f32) * normed).astype(bf16)


def total_kernel(own_ref, *refs):
    parts, (dk_ref, dv_ref) = refs[:7], refs[7:]
    total = own_ref[...]
    for part in parts:
        total = total + part[...].astype(f32)
    dk_ref[...] = total[:, :F].astype(bf16)
    dv_ref[...] = total[:, F:].astype(bf16)


def call(kernel, outs, smem=0):
    def run(*args):
        specs = [pl.BlockSpec(memory_space=pltpu.SMEM)] * smem + [VMEM] * (len(args) - smem)
        return pl.pallas_call(
            kernel,
            out_shape=[jax.ShapeDtypeStruct(s, t) for s, t in outs],
            in_specs=specs,
            out_specs=[VMEM] * len(outs),
            compiler_params=PARAMS,
        )(*args)

    return run


def shifted(x, by):
    count = lax.axis_size("seq")
    return lax.ppermute(x, "seq", [(i, i + by) for i in range(count) if 0 <= i + by < count])


def per_device(
    query_rows,
    key_rows,
    value_rows,
    gate_rows,
    cotangent,
    event_gaps,
    block_lists,
    bias_table,
    norm_gain,
):
    count = lax.axis_size("seq")
    group = lax.axis_index("seq").astype(i32).reshape(1)
    gain = norm_gain.reshape(1, F)
    packet, totals = pl.pallas_call(
        pack_kernel,
        out_shape=[
            jax.ShapeDtypeStruct((C + PAD, 2 * F), bf16),
            jax.ShapeDtypeStruct((ROW, 1, C), f32),
        ],
        in_specs=[pl.BlockSpec(memory_space=pltpu.HBM)] * 3,
        out_specs=[VMEM] * 2,
        scratch_shapes=[pltpu.VMEM((1, C), i32), pltpu.SemaphoreType.DMA((3,))],
        compiler_params=pltpu.CompilerParams(vmem_limit_bytes=60 * 1024 * 1024),
    )(key_rows, value_rows, event_gaps.reshape(1, C))
    rows = [[y * ROW + k for k in range(ROW)] for y in range(count // ROW)]
    totals = lax.all_to_all(totals, "seq", 0, 0, axis_index_groups=rows)
    fetched = {d: shifted(packet, d) for d in (16, 8, 4, 2, 1)}
    (row_packet,) = call(row_kernel, [((C + PAD, 2 * F), bf16)])(packet, totals)
    fetched |= {d: shifted(row_packet, d) for d in (64, 32)}
    heads, scaled, table, lists = call(
        prepare_kernel,
        [((2 * C, F), bf16), ((C, F), f32), ((2, C), f32), ((8, C), i32)],
    )(query_rows, gate_rows, cotangent, gain, bias_table, block_lists.T)
    packets = [packet] + [fetched[d] for d in DISTANCES]
    att, sums, weights, slopes = call(
        forward_kernel,
        [((C, F), f32), ((4, C), f32), ((2 * C, 8 * C), bf16), ((2 * C, 8 * C), f32)],
        1,
    )(group, heads, scaled, lists, table, totals, *packets)
    sums = lax.psum(sums, "head")
    kept = (heads, weights, slopes)
    sent = {}
    blocks = (5,)
    grads, acc, *parts = call(
        functools.partial(first_backward, blocks),
        [((2 * C, F), bf16), ((2 * C, F), f32)] + [((C, 2 * F), bf16)] * len(blocks),
    )(att, sums, heads, scaled, weights, slopes, *(packets[b] for b in blocks))
    sent |= dict(zip(blocks, parts))
    for blocks in ((4, 3), (7, 2, 6), (1,)):
        acc, *parts = call(
            functools.partial(next_backward, blocks),
            [((2 * C, F), f32)] + [((C, 2 * F), bf16)] * len(blocks),
        )(grads, acc, *kept, *(packets[b] for b in blocks))
        sent |= dict(zip(blocks, parts))
    returned = [shifted(part, -DISTANCES[b - 1]) for b, part in sent.items()]
    layer_out, grad_query, grad_gate, own = call(
        last_backward, [((C, F), bf16)] * 3 + [((C, 2 * F), f32)]
    )(grads, acc, *kept, packet, att, sums, gate_rows, cotangent, gain)
    grad_key, grad_value = call(total_kernel, [((C, F), bf16)] * 2)(own, *returned)
    return layer_out, grad_query, grad_key, grad_value, grad_gate


def solution(mesh):
    rows = P("seq", "head")
    return jax.shard_map(
        per_device,
        mesh=mesh,
        in_specs=(rows, rows, rows, rows, rows, P("seq"), P(), P("head", None), P("head")),
        out_specs=(rows, rows, rows, rows, rows),
        check_vma=False,
    )
```

```python
import functools

import jax
import jax.numpy as jnp
from jax import lax
from jax.experimental import pallas as pl
from jax.experimental.pallas import tpu as pltpu
from jax.sharding import PartitionSpec as P

norm_eps = 1e-05
C = 128
F = 128
DH = 64
DISTANCES = (1, 2, 4, 8, 16, 32, 64)
ROW = 32
PAD = 16
WIDE = 512.0
f32, bf16, i32 = jnp.float32, jnp.bfloat16, jnp.int32
VMEM = pl.BlockSpec(memory_space=pltpu.VMEM)
COST = pl.CostEstimate(flops=8 * 10**8, bytes_accessed=2**20, transcendentals=0)
PARAMS = pltpu.CompilerParams(vmem_limit_bytes=40 * 1024 * 1024)


def iota(shape, dim):
    return lax.broadcasted_iota(i32, shape, dim)


def by_head(rows):
    left = iota(rows.shape, 1) < DH
    zero = jnp.zeros_like(rows)
    return jnp.concatenate([jnp.where(left, rows, zero), jnp.where(left, zero, rows)], axis=0)


def from_heads(both):
    left = iota((C, F), 1) < DH
    return jnp.where(left, both[:C], both[C:])


def dot(a, b, dims, precision=None):
    return lax.dot_general(a, b, (dims, ((), ())), preferred_element_type=f32, precision=precision)


NN, NT, TN = ((1,), (0,)), ((1,), (1,)), ((0,), (0,))


def pack_kernel(key_ref, value_ref, gaps_ref, out_ref, totals_ref, gaps_buf, sems):
    copies = [
        pltpu.make_async_copy(gaps_ref, gaps_buf, sems.at[0]),
        pltpu.make_async_copy(key_ref, out_ref.at[pl.ds(0, C), pl.ds(0, F)], sems.at[1]),
        pltpu.make_async_copy(value_ref, out_ref.at[pl.ds(0, C), pl.ds(F, F)], sems.at[2]),
    ]
    for copy in copies:
        copy.start()
    copies[0].wait()
    gaps = gaps_buf[...].astype(f32)
    total = jnp.sum(gaps, axis=1, keepdims=True)
    totals_ref[...] = jnp.broadcast_to(total.reshape(1, 1, 1), (ROW, 1, C))
    gaps = jnp.broadcast_to(gaps, (PAD, C)).astype(bf16)
    out_ref[C:, :F] = gaps
    out_ref[C:, F:] = gaps
    copies[1].wait()
    copies[2].wait()


def row_kernel(packet_ref, totals_ref, out_ref):
    out_ref[:C, :] = packet_ref[:C, :]
    totals = totals_ref[...].reshape(ROW, C)
    totals = jnp.where(iota((ROW, C), 0) == iota((ROW, C), 1), totals, 0.0)
    totals = jnp.sum(totals, axis=0, keepdims=True)
    high = jnp.floor(totals * 0.0625)
    low = totals - 16.0 * high
    line = iota((PAD, C), 0)
    gaps = packet_ref[C:, :F].astype(f32)
    out_ref[C:, :F] = jnp.where(line == 1, high, jnp.where(line == 2, low, gaps)).astype(bf16)
    out_ref[C:, F:] = packet_ref[C:, F:]


def prepare_kernel(query_ref, gate_ref, cot_ref, gain_ref, table_ref, lists_ref, *outs):
    heads_ref, scaled_ref, table_out_ref, lists_out_ref = outs
    heads_ref[...] = by_head((query_ref[...].astype(f32) * 0.125).astype(bf16))
    scaled_ref[...] = cot_ref[...].astype(f32) * gate_ref[...].astype(f32) * gain_ref[...]
    table_out_ref[...] = jnp.pad(table_ref[...], ((0, 0), (0, C - 16)))
    lists_out_ref[...] = lists_ref[...]


def forward_kernel(group_ref, heads_ref, scaled_ref, lists_ref, table_ref, totals_ref, *refs):
    packets, (att_ref, sums_ref, weights_ref, slopes_ref) = refs[:8], refs[8:]
    group = group_ref[0]
    place = lax.rem(group, ROW)
    queries = heads_ref[...]
    gaps = jnp.concatenate([p[C : C + 1, :F] for p in packets], axis=0)
    upper = (iota((C, C), 0) <= iota((C, C), 1)).astype(bf16)
    key_times = dot(gaps, upper, NN)
    lower = (iota((C, C), 1) <= iota((C, C), 0)).astype(bf16)
    query_times = dot(lower, gaps, NT)[:, :1]
    own = totals_ref[...].reshape(ROW, C)
    own = jnp.where(iota((ROW, C), 0) == iota((ROW, C), 1), own, 0.0)
    totals = [jnp.sum(own, axis=0, keepdims=True)]
    for packet in packets[6:]:
        part = packet[C:, :F].astype(f32)
        totals.append(part[1:2, :] * 16.0 + part[2:3, :])
    lane = iota((8, C), 1)
    distance = jnp.left_shift(1, iota((8, C), 0)) >> 1
    between = jnp.zeros((8, C), f32)
    for r, total in enumerate(totals):
        back = place - lane + ROW * r
        inside = (back >= 1) & (back <= distance) & (lane < ROW)
        between = between + jnp.where(inside, total, 0.0)
    shifts = jnp.sum(between, axis=1, keepdims=True) - key_times
    listed = jnp.where(lane == group, lists_ref[...], 0)
    listed = jnp.sum(listed.astype(f32), axis=1, keepdims=True) >= 0.0
    listed = listed.astype(f32)
    tables = [jnp.broadcast_to(table_ref[h : h + 1, :], (C, C)) for h in range(2)]
    acc = jnp.zeros((2 * C, F), f32)
    for b, packet in enumerate(packets):
        scores = dot(queries, packet[:C, :F], NT)
        delta = (query_times + shifts[b : b + 1, :]).astype(i32)
        bucket = jnp.minimum(32 - lax.clz(delta), 15)
        bias = jnp.concatenate([jnp.take_along_axis(t, bucket, axis=1) for t in tables], axis=0)
        scores = scores + bias
        sig = 0.5 * jnp.tanh(0.5 * scores) + 0.5
        silu = scores * sig
        slope = sig + silu * (1.0 - sig)
        if b == 0:
            keep = (iota((C, C), 1) <= iota((C, C), 0)).astype(f32)
            keep = jnp.concatenate([keep, keep], axis=0)
        else:
            keep = listed[b - 1 : b, :]
        weights = (silu * keep).astype(bf16)
        weights_ref[:, b * C : (b + 1) * C] = weights
        slopes_ref[:, b * C : (b + 1) * C] = slope * keep
        acc = acc + dot(weights, packet[:C, F:], NN)
    att = from_heads(acc)
    att_ref[...] = att
    scaled = scaled_ref[...]
    terms = jnp.concatenate([att, att * att, scaled, scaled * att], axis=0)
    rows = dot(jnp.ones((8, F), f32), terms, NT, lax.Precision.HIGHEST)
    for r in range(4):
        sums_ref[r : r + 1, :] = rows[0:1, r * C : (r + 1) * C]


def norm_terms(sums_ref, att_ref):
    sums = jnp.concatenate([sums_ref[...], jnp.zeros((4, C), f32)], axis=0)
    cols = jnp.transpose(sums) * (1.0 / WIDE)
    mean, square, mean_scaled, mean_cross = (cols[:, r : r + 1] for r in range(4))
    inv_std = lax.rsqrt(square - mean * mean + norm_eps)
    mean_cross = (mean_cross - mean * mean_scaled) * inv_std
    return inv_std, (att_ref[...] - mean) * inv_std, mean_scaled, mean_cross


def add_kernel(part_ref, received_ref, out_ref):
    out_ref[...] = (part_ref[...] + received_ref[...].astype(f32)).astype(bf16)


def block_grads(b, queries, grads, weights_ref, slopes_ref, packet, out_ref):
    at = slice(b * C, (b + 1) * C)
    grad_weights = dot(grads, packet[:C, F:], NT)
    grad_scores = (grad_weights * slopes_ref[:, at]).astype(bf16)
    out_ref[:, :F] = dot(grad_scores, queries, TN).astype(out_ref.dtype)
    out_ref[:, F:] = dot(weights_ref[:, at], grads, TN).astype(out_ref.dtype)
    return dot(grad_scores, packet[:C, :F], NN)


def first_backward(blocks, att_ref, sums_ref, heads_ref, scaled_ref, weights_ref, slopes_ref, *refs):
    n = len(blocks)
    packets, grads_ref, acc_ref, sent = refs[:n], refs[n], refs[n + 1], refs[n + 2 :]
    inv_std, centered, mean_scaled, mean_cross = norm_terms(sums_ref, att_ref)
    grads = inv_std * (scaled_ref[...] - mean_scaled - centered * mean_cross)
    grads = by_head(grads.astype(bf16))
    grads_ref[...] = grads
    queries = heads_ref[...]
    acc = jnp.zeros((2 * C, F), f32)
    for b, packet, out in zip(blocks, packets, sent):
        acc = acc + block_grads(b, queries, grads, weights_ref, slopes_ref, packet, out)
    acc_ref[...] = acc


def next_backward(blocks, grads_ref, before_ref, heads_ref, weights_ref, slopes_ref, *refs):
    n = len(blocks)
    packets, acc_ref, sent = refs[:n], refs[n], refs[n + 1 :]
    grads, queries, acc = grads_ref[...], heads_ref[...], before_ref[...]
    for b, packet, out in zip(blocks, packets, sent):
        acc = acc + block_grads(b, queries, grads, weights_ref, slopes_ref, packet, out)
    acc_ref[...] = acc


def last_backward(
    grads_ref, before_ref, heads_ref, weights_ref, slopes_ref, packet, att_ref, sums_ref, gate_ref, cot_ref, gain_ref, *outs
):
    out_ref, dq_ref, dgate_ref, own_ref = outs
    acc = before_ref[...] + block_grads(
        0, heads_ref[...], grads_ref[...], weights_ref, slopes_ref, packet, own_ref
    )
    dq_ref[...] = (from_heads(acc) * 0.125).astype(bf16)
    centered = norm_terms(sums_ref, att_ref)[1]
    normed = centered * gain_ref[...]
    out_ref[...] = (normed * gate_ref[...].astype(f32)).astype(bf16)
    dgate_ref[...] = (cot_ref[...].astype(f32) * normed).astype(bf16)


def total_kernel(own_ref, *refs):
    parts, (dk_ref, dv_ref) = refs[:-2], refs[-2:]
    total = own_ref[...]
    for part in parts:
        total = total + part[...].astype(f32)
    dk_ref[...] = total[:, :F].astype(bf16)
    dv_ref[...] = total[:, F:].astype(bf16)


def call(kernel, outs, smem=0, cost=None):
    def run(*args):
        specs = [pl.BlockSpec(memory_space=pltpu.SMEM)] * smem + [VMEM] * (len(args) - smem)
        return pl.pallas_call(
            kernel,
            out_shape=[jax.ShapeDtypeStruct(s, t) for s, t in outs],
            in_specs=specs,
            out_specs=[VMEM] * len(outs),
            compiler_params=PARAMS,
            cost_estimate=cost,
        )(*args)

    return run


def shifted(x, by):
    count = lax.axis_size("seq")
    return lax.ppermute(x, "seq", [(i, i + by) for i in range(count) if 0 <= i + by < count])


def per_device(
    query_rows,
    key_rows,
    value_rows,
    gate_rows,
    cotangent,
    event_gaps,
    block_lists,
    bias_table,
    norm_gain,
):
    count = lax.axis_size("seq")
    group = lax.axis_index("seq").astype(i32).reshape(1)
    gain = norm_gain.reshape(1, F)
    packet, totals = pl.pallas_call(
        pack_kernel,
        out_shape=[
            jax.ShapeDtypeStruct((C + PAD, 2 * F), bf16),
            jax.ShapeDtypeStruct((ROW, 1, C), f32),
        ],
        in_specs=[pl.BlockSpec(memory_space=pltpu.HBM)] * 3,
        out_specs=[VMEM] * 2,
        scratch_shapes=[pltpu.VMEM((1, C), i32), pltpu.SemaphoreType.DMA((3,))],
        compiler_params=pltpu.CompilerParams(vmem_limit_bytes=60 * 1024 * 1024),
    )(key_rows, value_rows, event_gaps.reshape(1, C))
    rows = [[y * ROW + k for k in range(ROW)] for y in range(count // ROW)]
    totals = lax.all_to_all(totals, "seq", 0, 0, axis_index_groups=rows)
    fetched = {d: shifted(packet, d) for d in (16, 8, 4, 2, 1)}
    (row_packet,) = call(row_kernel, [((C + PAD, 2 * F), bf16)])(packet, totals)
    fetched |= {d: shifted(row_packet, d) for d in (64, 32)}
    heads, scaled, table, lists = call(
        prepare_kernel,
        [((2 * C, F), bf16), ((C, F), f32), ((2, C), f32), ((8, C), i32)],
    )(query_rows, gate_rows, cotangent, gain, bias_table, block_lists.T)
    packets = [packet] + [fetched[d] for d in DISTANCES]
    att, sums, weights, slopes = call(
        forward_kernel,
        [((C, F), f32), ((4, C), f32), ((2 * C, 8 * C), bf16), ((2 * C, 8 * C), f32)],
        1,
    )(group, heads, scaled, lists, table, totals, *packets)
    sums = lax.psum(sums, "head")
    kept = (heads, weights, slopes)
    narrow, wide = ((C, 2 * F), bf16), ((C, 2 * F), f32)
    blocks = (5, 4)
    grads, acc, part16, part8 = call(
        functools.partial(first_backward, blocks),
        [((2 * C, F), bf16), ((2 * C, F), f32), narrow, narrow],
    )(att, sums, heads, scaled, weights, slopes, *(packets[b] for b in blocks))

    def more(blocks, acc, outs):
        return call(functools.partial(next_backward, blocks), [((2 * C, F), f32)] + outs, cost=COST)(
            grads, acc, *kept, *(packets[b] for b in blocks)
        )

    relayed = shifted(part8, -4)
    acc, part64, part32, part2, part1, part4 = more((7, 6, 2, 1, 3), acc, [narrow] * 4 + [wide])
    returned = [
        shifted(part16, -16),
        shifted(part64, -64),
        shifted(part32, -32),
        shifted(part2, -2),
        shifted(part1, -1),
    ]
    part4, relayed, returned[0] = lax.optimization_barrier((part4, relayed, returned[0]))
    (both,) = call(add_kernel, [narrow])(part4, relayed)
    returned.append(shifted(both, -4))
    layer_out, grad_query, grad_gate, own = call(
        last_backward, [((C, F), bf16)] * 3 + [((C, 2 * F), f32)]
    )(grads, acc, *kept, packet, att, sums, gate_rows, cotangent, gain)
    grad_key, grad_value = call(total_kernel, [((C, F), bf16)] * 2)(own, *returned)
    return layer_out, grad_query, grad_key, grad_value, grad_gate


def solution(mesh):
    rows = P("seq", "head")
    return jax.shard_map(
        per_device,
        mesh=mesh,
        in_specs=(rows, rows, rows, rows, rows, P("seq"), P(), P("head", None), P("head")),
        out_specs=(rows, rows, rows, rows, rows),
        check_vma=False,
    )
```

```python
import functools

import jax
import jax.numpy as jnp
from jax import lax
from jax.experimental import pallas as pl
from jax.experimental.pallas import tpu as pltpu
from jax.sharding import PartitionSpec as P

norm_eps = 1e-05
C = 128
F = 128
DH = 64
DISTANCES = (1, 2, 4, 8, 16, 32, 64)
ROW = 32
PAD = 16
WIDE = 512.0
f32, bf16, i32 = jnp.float32, jnp.bfloat16, jnp.int32
VMEM = pl.BlockSpec(memory_space=pltpu.VMEM)
COST = pl.CostEstimate(flops=8 * 10**8, bytes_accessed=2**20, transcendentals=0)
PARAMS = pltpu.CompilerParams(vmem_limit_bytes=40 * 1024 * 1024)


def iota(shape, dim):
    return lax.broadcasted_iota(i32, shape, dim)


def by_head(rows):
    left = iota(rows.shape, 1) < DH
    zero = jnp.zeros_like(rows)
    return jnp.concatenate([jnp.where(left, rows, zero), jnp.where(left, zero, rows)], axis=0)


def from_heads(both):
    left = iota((C, F), 1) < DH
    return jnp.where(left, both[:C], both[C:])


def dot(a, b, dims, precision=None):
    return lax.dot_general(a, b, (dims, ((), ())), preferred_element_type=f32, precision=precision)


NN, NT, TN = ((1,), (0,)), ((1,), (1,)), ((0,), (0,))


def pack_kernel(key_ref, value_ref, gaps_ref, out_ref, totals_ref, gaps_buf, sems):
    copies = [
        pltpu.make_async_copy(gaps_ref, gaps_buf, sems.at[0]),
        pltpu.make_async_copy(key_ref, out_ref.at[pl.ds(0, C), pl.ds(0, F)], sems.at[1]),
        pltpu.make_async_copy(value_ref, out_ref.at[pl.ds(0, C), pl.ds(F, F)], sems.at[2]),
    ]
    for copy in copies:
        copy.start()
    copies[0].wait()
    gaps = gaps_buf[...].astype(f32)
    total = jnp.sum(gaps, axis=1, keepdims=True)
    totals_ref[...] = jnp.broadcast_to(total.reshape(1, 1, 1), (ROW, 1, C))
    gaps = jnp.broadcast_to(gaps, (PAD, C)).astype(bf16)
    out_ref[C:, :F] = gaps
    out_ref[C:, F:] = gaps
    copies[1].wait()
    copies[2].wait()


def row_kernel(packet_ref, totals_ref, out_ref):
    out_ref[:C, :] = packet_ref[:C, :]
    totals = totals_ref[...].reshape(ROW, C)
    totals = jnp.where(iota((ROW, C), 0) == iota((ROW, C), 1), totals, 0.0)
    totals = jnp.sum(totals, axis=0, keepdims=True)
    high = jnp.floor(totals * 0.0625)
    low = totals - 16.0 * high
    line = iota((PAD, C), 0)
    gaps = packet_ref[C:, :F].astype(f32)
    out_ref[C:, :F] = jnp.where(line == 1, high, jnp.where(line == 2, low, gaps)).astype(bf16)
    out_ref[C:, F:] = packet_ref[C:, F:]


def prepare_kernel(query_ref, gate_ref, cot_ref, gain_ref, table_ref, lists_ref, *outs):
    heads_ref, scaled_ref, table_out_ref, lists_out_ref = outs
    heads_ref[...] = by_head((query_ref[...].astype(f32) * 0.125).astype(bf16))
    scaled_ref[...] = cot_ref[...].astype(f32) * gate_ref[...].astype(f32) * gain_ref[...]
    table_out_ref[...] = jnp.pad(table_ref[...], ((0, 0), (0, C - 16)))
    lists_out_ref[...] = lists_ref[...]


def forward_kernel(group_ref, heads_ref, scaled_ref, lists_ref, table_ref, totals_ref, *refs):
    packets, (att_ref, sums_ref, weights_ref, slopes_ref) = refs[:8], refs[8:]
    group = group_ref[0]
    place = lax.rem(group, ROW)
    queries = heads_ref[...]
    gaps = jnp.concatenate([p[C : C + 1, :F] for p in packets], axis=0)
    upper = (iota((C, C), 0) <= iota((C, C), 1)).astype(bf16)
    key_times = dot(gaps, upper, NN)
    lower = (iota((C, C), 1) <= iota((C, C), 0)).astype(bf16)
    query_times = dot(lower, gaps, NT)[:, :1]
    own = totals_ref[...].reshape(ROW, C)
    own = jnp.where(iota((ROW, C), 0) == iota((ROW, C), 1), own, 0.0)
    totals = [jnp.sum(own, axis=0, keepdims=True)]
    for packet in packets[6:]:
        part = packet[C:, :F].astype(f32)
        totals.append(part[1:2, :] * 16.0 + part[2:3, :])
    lane = iota((8, C), 1)
    distance = jnp.left_shift(1, iota((8, C), 0)) >> 1
    between = jnp.zeros((8, C), f32)
    for r, total in enumerate(totals):
        back = place - lane + ROW * r
        inside = (back >= 1) & (back <= distance) & (lane < ROW)
        between = between + jnp.where(inside, total, 0.0)
    shifts = jnp.sum(between, axis=1, keepdims=True) - key_times
    listed = jnp.where(lane == group, lists_ref[...], 0)
    listed = jnp.sum(listed.astype(f32), axis=1, keepdims=True) >= 0.0
    listed = listed.astype(f32)
    tables = [jnp.broadcast_to(table_ref[h : h + 1, :], (C, C)) for h in range(2)]
    acc = jnp.zeros((2 * C, F), f32)
    for b, packet in enumerate(packets):
        scores = dot(queries, packet[:C, :F], NT)
        delta = (query_times + shifts[b : b + 1, :]).astype(i32)
        bucket = jnp.minimum(32 - lax.clz(delta), 15)
        bias = jnp.concatenate([jnp.take_along_axis(t, bucket, axis=1) for t in tables], axis=0)
        scores = scores + bias
        sig = 0.5 * jnp.tanh(0.5 * scores) + 0.5
        silu = scores * sig
        slope = sig + silu * (1.0 - sig)
        if b == 0:
            keep = (iota((C, C), 1) <= iota((C, C), 0)).astype(f32)
            keep = jnp.concatenate([keep, keep], axis=0)
        else:
            keep = listed[b - 1 : b, :]
        weights = (silu * keep).astype(bf16)
        weights_ref[:, b * C : (b + 1) * C] = weights
        slopes_ref[:, b * C : (b + 1) * C] = slope * keep
        acc = acc + dot(weights, packet[:C, F:], NN)
    att = from_heads(acc)
    att_ref[...] = att
    scaled = scaled_ref[...]
    terms = jnp.concatenate([att, att * att, scaled, scaled * att], axis=0)
    rows = dot(jnp.ones((8, F), f32), terms, NT, lax.Precision.HIGHEST)
    for r in range(4):
        for x in range(4):
            sums_ref[x, r : r + 1, :] = rows[0:1, r * C : (r + 1) * C]


def norm_terms(sums_ref, att_ref):
    sums = sums_ref[0] + sums_ref[1] + sums_ref[2] + sums_ref[3]
    sums = jnp.concatenate([sums, jnp.zeros((4, C), f32)], axis=0)
    cols = jnp.transpose(sums) * (1.0 / WIDE)
    mean, square, mean_scaled, mean_cross = (cols[:, r : r + 1] for r in range(4))
    inv_std = lax.rsqrt(square - mean * mean + norm_eps)
    mean_cross = (mean_cross - mean * mean_scaled) * inv_std
    return inv_std, (att_ref[...] - mean) * inv_std, mean_scaled, mean_cross


def add_kernel(part_ref, received_ref, out_ref):
    out_ref[...] = (part_ref[...] + received_ref[...].astype(f32)).astype(bf16)


def block_grads(b, queries, grads, weights_ref, slopes_ref, packet, out_ref):
    at = slice(b * C, (b + 1) * C)
    grad_weights = dot(grads, packet[:C, F:], NT)
    grad_scores = (grad_weights * slopes_ref[:, at]).astype(bf16)
    out_ref[:, :F] = dot(grad_scores, queries, TN).astype(out_ref.dtype)
    out_ref[:, F:] = dot(weights_ref[:, at], grads, TN).astype(out_ref.dtype)
    return dot(grad_scores, packet[:C, :F], NN)


def first_backward(blocks, att_ref, sums_ref, heads_ref, scaled_ref, weights_ref, slopes_ref, *refs):
    n = len(blocks)
    packets, grads_ref, acc_ref, sent = refs[:n], refs[n], refs[n + 1], refs[n + 2 :]
    inv_std, centered, mean_scaled, mean_cross = norm_terms(sums_ref, att_ref)
    grads = inv_std * (scaled_ref[...] - mean_scaled - centered * mean_cross)
    grads = by_head(grads.astype(bf16))
    grads_ref[...] = grads
    queries = heads_ref[...]
    acc = jnp.zeros((2 * C, F), f32)
    for b, packet, out in zip(blocks, packets, sent):
        acc = acc + block_grads(b, queries, grads, weights_ref, slopes_ref, packet, out)
    acc_ref[...] = acc


def next_backward(blocks, grads_ref, before_ref, heads_ref, weights_ref, slopes_ref, *refs):
    n = len(blocks)
    packets, acc_ref, sent = refs[:n], refs[n], refs[n + 1 :]
    grads, queries, acc = grads_ref[...], heads_ref[...], before_ref[...]
    for b, packet, out in zip(blocks, packets, sent):
        acc = acc + block_grads(b, queries, grads, weights_ref, slopes_ref, packet, out)
    acc_ref[...] = acc


def last_backward(
    grads_ref, before_ref, heads_ref, weights_ref, slopes_ref, packet, att_ref, sums_ref, gate_ref, cot_ref, gain_ref, *outs
):
    out_ref, dq_ref, dgate_ref, own_ref = outs
    acc = before_ref[...] + block_grads(
        0, heads_ref[...], grads_ref[...], weights_ref, slopes_ref, packet, own_ref
    )
    dq_ref[...] = (from_heads(acc) * 0.125).astype(bf16)
    centered = norm_terms(sums_ref, att_ref)[1]
    normed = centered * gain_ref[...]
    out_ref[...] = (normed * gate_ref[...].astype(f32)).astype(bf16)
    dgate_ref[...] = (cot_ref[...].astype(f32) * normed).astype(bf16)


def total_kernel(own_ref, *refs):
    parts, (dk_ref, dv_ref) = refs[:-2], refs[-2:]
    total = own_ref[...]
    for part in parts:
        total = total + part[...].astype(f32)
    dk_ref[...] = total[:, :F].astype(bf16)
    dv_ref[...] = total[:, F:].astype(bf16)


def call(kernel, outs, smem=0, cost=None):
    def run(*args):
        specs = [pl.BlockSpec(memory_space=pltpu.SMEM)] * smem + [VMEM] * (len(args) - smem)
        return pl.pallas_call(
            kernel,
            out_shape=[jax.ShapeDtypeStruct(s, t) for s, t in outs],
            in_specs=specs,
            out_specs=[VMEM] * len(outs),
            compiler_params=PARAMS,
            cost_estimate=cost,
        )(*args)

    return run


def shifted(x, by):
    count = lax.axis_size("seq")
    return lax.ppermute(x, "seq", [(i, i + by) for i in range(count) if 0 <= i + by < count])


def per_device(
    query_rows,
    key_rows,
    value_rows,
    gate_rows,
    cotangent,
    event_gaps,
    block_lists,
    bias_table,
    norm_gain,
):
    count = lax.axis_size("seq")
    group = lax.axis_index("seq").astype(i32).reshape(1)
    gain = norm_gain.reshape(1, F)
    packet, totals = pl.pallas_call(
        pack_kernel,
        out_shape=[
            jax.ShapeDtypeStruct((C + PAD, 2 * F), bf16),
            jax.ShapeDtypeStruct((ROW, 1, C), f32),
        ],
        in_specs=[pl.BlockSpec(memory_space=pltpu.HBM)] * 3,
        out_specs=[VMEM] * 2,
        scratch_shapes=[pltpu.VMEM((1, C), i32), pltpu.SemaphoreType.DMA((3,))],
        compiler_params=pltpu.CompilerParams(vmem_limit_bytes=60 * 1024 * 1024),
    )(key_rows, value_rows, event_gaps.reshape(1, C))
    rows = [[y * ROW + k for k in range(ROW)] for y in range(count // ROW)]
    totals = lax.all_to_all(totals, "seq", 0, 0, axis_index_groups=rows)
    fetched = {d: shifted(packet, d) for d in (16, 8, 4, 2, 1)}
    (row_packet,) = call(row_kernel, [((C + PAD, 2 * F), bf16)])(packet, totals)
    fetched |= {d: shifted(row_packet, d) for d in (64, 32)}
    heads, scaled, table, lists = call(
        prepare_kernel,
        [((2 * C, F), bf16), ((C, F), f32), ((2, C), f32), ((8, C), i32)],
    )(query_rows, gate_rows, cotangent, gain, bias_table, block_lists.T)
    packets = [packet] + [fetched[d] for d in DISTANCES]
    att, sums, weights, slopes = call(
        forward_kernel,
        [((C, F), f32), ((4, 4, C), f32), ((2 * C, 8 * C), bf16), ((2 * C, 8 * C), f32)],
        1,
    )(group, heads, scaled, lists, table, totals, *packets)
    sums = lax.all_to_all(sums, "head", 0, 0)
    kept = (heads, weights, slopes)
    narrow, wide = ((C, 2 * F), bf16), ((C, 2 * F), f32)
    blocks = (5, 7, 4, 3, 6, 2, 1)
    grads, acc, *parts = call(
        functools.partial(first_backward, blocks),
        [((2 * C, F), bf16), ((2 * C, F), f32)] + [narrow] * 7,
    )(att, sums, heads, scaled, weights, slopes, *(packets[b] for b in blocks))
    returned = [shifted(part, -DISTANCES[b - 1]) for b, part in zip(blocks, parts)]
    layer_out, grad_query, grad_gate, own = call(
        last_backward, [((C, F), bf16)] * 3 + [((C, 2 * F), f32)]
    )(grads, acc, *kept, packet, att, sums, gate_rows, cotangent, gain)
    grad_key, grad_value = call(total_kernel, [((C, F), bf16)] * 2)(own, *returned)
    return layer_out, grad_query, grad_key, grad_value, grad_gate


def solution(mesh):
    rows = P("seq", "head")
    return jax.shard_map(
        per_device,
        mesh=mesh,
        in_specs=(rows, rows, rows, rows, rows, P("seq"), P(), P("head", None), P("head")),
        out_specs=(rows, rows, rows, rows, rows),
        check_vma=False,
    )
```

```python
import functools

import jax
import jax.numpy as jnp
from jax import lax
from jax.experimental import pallas as pl
from jax.experimental.pallas import tpu as pltpu
from jax.sharding import PartitionSpec as P

norm_eps = 1e-05
C = 128
F = 128
DH = 64
DISTANCES = (1, 2, 4, 8, 16, 32, 64)
ROW = 32
PAD = 16
WIDE = 512.0
f32, bf16, i32 = jnp.float32, jnp.bfloat16, jnp.int32
VMEM = pl.BlockSpec(memory_space=pltpu.VMEM)
PARAMS = pltpu.CompilerParams(vmem_limit_bytes=40 * 1024 * 1024)


def iota(shape, dim):
    return lax.broadcasted_iota(i32, shape, dim)


def by_head(rows):
    left = iota(rows.shape, 1) < DH
    zero = jnp.zeros_like(rows)
    return jnp.concatenate([jnp.where(left, rows, zero), jnp.where(left, zero, rows)], axis=0)


def from_heads(both):
    left = iota((C, F), 1) < DH
    return jnp.where(left, both[:C], both[C:])


def dot(a, b, dims, precision=None):
    return lax.dot_general(a, b, (dims, ((), ())), preferred_element_type=f32, precision=precision)


NN, NT, TN = ((1,), (0,)), ((1,), (1,)), ((0,), (0,))


def pack_kernel(key_ref, value_ref, gaps_ref, out_ref, totals_ref, gaps_buf, sems):
    copies = [
        pltpu.make_async_copy(gaps_ref, gaps_buf, sems.at[0]),
        pltpu.make_async_copy(key_ref, out_ref.at[pl.ds(0, C), pl.ds(0, F)], sems.at[1]),
        pltpu.make_async_copy(value_ref, out_ref.at[pl.ds(0, C), pl.ds(F, F)], sems.at[2]),
    ]
    for copy in copies:
        copy.start()
    copies[0].wait()
    gaps = gaps_buf[...].astype(f32)
    total = jnp.sum(gaps, axis=1, keepdims=True)
    totals_ref[...] = jnp.broadcast_to(total.reshape(1, 1, 1), (ROW, 1, C))
    gaps = jnp.broadcast_to(gaps, (PAD, C)).astype(bf16)
    out_ref[C:, :F] = gaps
    out_ref[C:, F:] = gaps
    copies[1].wait()
    copies[2].wait()


def row_kernel(packet_ref, totals_ref, out_ref):
    out_ref[:C, :] = packet_ref[:C, :]
    totals = totals_ref[...].reshape(ROW, C)
    totals = jnp.where(iota((ROW, C), 0) == iota((ROW, C), 1), totals, 0.0)
    totals = jnp.sum(totals, axis=0, keepdims=True)
    high = jnp.floor(totals * 0.0625)
    low = totals - 16.0 * high
    line = iota((PAD, C), 0)
    gaps = packet_ref[C:, :F].astype(f32)
    out_ref[C:, :F] = jnp.where(line == 1, high, jnp.where(line == 2, low, gaps)).astype(bf16)
    out_ref[C:, F:] = packet_ref[C:, F:]


def prepare_kernel(query_ref, gate_ref, cot_ref, gain_ref, table_ref, lists_ref, *outs):
    heads_ref, scaled_ref, table_out_ref, lists_out_ref = outs
    heads_ref[...] = by_head((query_ref[...].astype(f32) * 0.125).astype(bf16))
    scaled_ref[...] = cot_ref[...].astype(f32) * gate_ref[...].astype(f32) * gain_ref[...]
    table_out_ref[...] = jnp.pad(table_ref[...], ((0, 0), (0, C - 16)))
    lists_out_ref[...] = lists_ref[...]


def forward_kernel(group_ref, heads_ref, scaled_ref, lists_ref, table_ref, totals_ref, *refs):
    packets, (att_ref, sums_ref, weights_ref, slopes_ref) = refs[:8], refs[8:]
    group = group_ref[0]
    place = lax.rem(group, ROW)
    queries = heads_ref[...]
    gaps = jnp.concatenate([p[C : C + 1, :F] for p in packets], axis=0)
    upper = (iota((C, C), 0) <= iota((C, C), 1)).astype(bf16)
    key_times = dot(gaps, upper, NN)
    lower = (iota((C, C), 1) <= iota((C, C), 0)).astype(bf16)
    query_times = dot(lower, gaps, NT)[:, :1]
    own = totals_ref[...].reshape(ROW, C)
    own = jnp.where(iota((ROW, C), 0) == iota((ROW, C), 1), own, 0.0)
    totals = [jnp.sum(own, axis=0, keepdims=True)]
    for packet in packets[6:]:
        part = packet[C:, :F].astype(f32)
        totals.append(part[1:2, :] * 16.0 + part[2:3, :])
    lane = iota((8, C), 1)
    distance = jnp.left_shift(1, iota((8, C), 0)) >> 1
    between = jnp.zeros((8, C), f32)
    for r, total in enumerate(totals):
        back = place - lane + ROW * r
        inside = (back >= 1) & (back <= distance) & (lane < ROW)
        between = between + jnp.where(inside, total, 0.0)
    shifts = jnp.sum(between, axis=1, keepdims=True) - key_times
    listed = jnp.where(lane == group, lists_ref[...], 0)
    listed = jnp.sum(listed.astype(f32), axis=1, keepdims=True) >= 0.0
    listed = listed.astype(f32)
    tables = [jnp.broadcast_to(table_ref[h : h + 1, :], (C, C)) for h in range(2)]
    acc = jnp.zeros((2 * C, F), f32)
    for b, packet in enumerate(packets):
        scores = dot(queries, packet[:C, :F], NT)
        delta = (query_times + shifts[b : b + 1, :]).astype(i32)
        bucket = jnp.minimum(32 - lax.clz(delta), 15)
        bias = jnp.concatenate([jnp.take_along_axis(t, bucket, axis=1) for t in tables], axis=0)
        scores = scores + bias
        sig = 0.5 * jnp.tanh(0.5 * scores) + 0.5
        silu = scores * sig
        slope = sig + silu * (1.0 - sig)
        if b == 0:
            keep = (iota((C, C), 1) <= iota((C, C), 0)).astype(f32)
            keep = jnp.concatenate([keep, keep], axis=0)
        else:
            keep = listed[b - 1 : b, :]
        weights = (silu * keep).astype(bf16)
        weights_ref[:, b * C : (b + 1) * C] = weights
        slopes_ref[:, b * C : (b + 1) * C] = slope * keep
        acc = acc + dot(weights, packet[:C, F:], NN)
    att = from_heads(acc)
    att_ref[...] = att
    scaled = scaled_ref[...]
    terms = jnp.concatenate([att, att * att, scaled, scaled * att], axis=0)
    rows = dot(jnp.ones((8, F), f32), terms, NT, lax.Precision.HIGHEST)
    for r in range(4):
        for x in range(4):
            sums_ref[x, r : r + 1, :] = rows[0:1, r * C : (r + 1) * C]


def norm_terms(sums_ref, att_ref):
    sums = sums_ref[0] + sums_ref[1] + sums_ref[2] + sums_ref[3]
    sums = jnp.concatenate([sums, jnp.zeros((4, C), f32)], axis=0)
    cols = jnp.transpose(sums) * (1.0 / WIDE)
    mean, square, mean_scaled, mean_cross = (cols[:, r : r + 1] for r in range(4))
    inv_std = lax.rsqrt(square - mean * mean + norm_eps)
    mean_cross = (mean_cross - mean * mean_scaled) * inv_std
    return inv_std, (att_ref[...] - mean) * inv_std, mean_scaled, mean_cross


def block_grads(b, queries, grads, weights_ref, slopes_ref, packet, out_ref):
    at = slice(b * C, (b + 1) * C)
    grad_weights = dot(grads, packet[:C, F:], NT)
    grad_scores = (grad_weights * slopes_ref[:, at]).astype(bf16)
    out_ref[:, :F] = dot(grad_scores, queries, TN).astype(out_ref.dtype)
    out_ref[:, F:] = dot(weights_ref[:, at], grads, TN).astype(out_ref.dtype)
    return dot(grad_scores, packet[:C, :F], NN)


def blocks_backward(blocks, att_ref, sums_ref, heads_ref, scaled_ref, weights_ref, slopes_ref, *refs):
    n = len(blocks)
    packets, grads_ref, acc_ref, sent = refs[:n], refs[n], refs[n + 1], refs[n + 2 :]
    inv_std, centered, mean_scaled, mean_cross = norm_terms(sums_ref, att_ref)
    grads = inv_std * (scaled_ref[...] - mean_scaled - centered * mean_cross)
    grads = by_head(grads.astype(bf16))
    grads_ref[...] = grads
    queries = heads_ref[...]
    acc = jnp.zeros((2 * C, F), f32)
    for b, packet, out in zip(blocks, packets, sent):
        acc = acc + block_grads(b, queries, grads, weights_ref, slopes_ref, packet, out)
    acc_ref[...] = acc


def last_backward(
    grads_ref, before_ref, heads_ref, weights_ref, slopes_ref, packet, att_ref, sums_ref, gate_ref, cot_ref, gain_ref, *outs
):
    out_ref, dq_ref, dgate_ref, own_ref = outs
    acc = before_ref[...] + block_grads(
        0, heads_ref[...], grads_ref[...], weights_ref, slopes_ref, packet, own_ref
    )
    dq_ref[...] = (from_heads(acc) * 0.125).astype(bf16)
    centered = norm_terms(sums_ref, att_ref)[1]
    normed = centered * gain_ref[...]
    out_ref[...] = (normed * gate_ref[...].astype(f32)).astype(bf16)
    dgate_ref[...] = (cot_ref[...].astype(f32) * normed).astype(bf16)


def total_kernel(own_ref, *refs):
    parts, (dk_ref, dv_ref) = refs[:-2], refs[-2:]
    total = own_ref[...]
    for part in parts:
        total = total + part[...].astype(f32)
    dk_ref[...] = total[:, :F].astype(bf16)
    dv_ref[...] = total[:, F:].astype(bf16)


def call(kernel, outs, smem=0):
    def run(*args):
        specs = [pl.BlockSpec(memory_space=pltpu.SMEM)] * smem + [VMEM] * (len(args) - smem)
        return pl.pallas_call(
            kernel,
            out_shape=[jax.ShapeDtypeStruct(s, t) for s, t in outs],
            in_specs=specs,
            out_specs=[VMEM] * len(outs),
            compiler_params=PARAMS,
        )(*args)

    return run


def shifted(x, by):
    count = lax.axis_size("seq")
    return lax.ppermute(x, "seq", [(i, i + by) for i in range(count) if 0 <= i + by < count])


def per_device(
    query_rows,
    key_rows,
    value_rows,
    gate_rows,
    cotangent,
    event_gaps,
    block_lists,
    bias_table,
    norm_gain,
):
    count = lax.axis_size("seq")
    group = lax.axis_index("seq").astype(i32).reshape(1)
    gain = norm_gain.reshape(1, F)
    packet, totals = pl.pallas_call(
        pack_kernel,
        out_shape=[
            jax.ShapeDtypeStruct((C + PAD, 2 * F), bf16),
            jax.ShapeDtypeStruct((ROW, 1, C), f32),
        ],
        in_specs=[pl.BlockSpec(memory_space=pltpu.HBM)] * 3,
        out_specs=[VMEM] * 2,
        scratch_shapes=[pltpu.VMEM((1, C), i32), pltpu.SemaphoreType.DMA((3,))],
        compiler_params=pltpu.CompilerParams(vmem_limit_bytes=60 * 1024 * 1024),
    )(key_rows, value_rows, event_gaps.reshape(1, C))
    rows = [[y * ROW + k for k in range(ROW)] for y in range(count // ROW)]
    totals = lax.all_to_all(totals, "seq", 0, 0, axis_index_groups=rows)
    fetched = {d: shifted(packet, d) for d in (16, 8, 4, 2, 1)}
    (row_packet,) = call(row_kernel, [((C + PAD, 2 * F), bf16)])(packet, totals)
    fetched |= {d: shifted(row_packet, d) for d in (64, 32)}
    heads, scaled, table, lists = call(
        prepare_kernel,
        [((2 * C, F), bf16), ((C, F), f32), ((2, C), f32), ((8, C), i32)],
    )(query_rows, gate_rows, cotangent, gain, bias_table, block_lists.T)
    packets = [packet] + [fetched[d] for d in DISTANCES]
    att, sums, weights, slopes = call(
        forward_kernel,
        [((C, F), f32), ((4, 4, C), f32), ((2 * C, 8 * C), bf16), ((2 * C, 8 * C), f32)],
        1,
    )(group, heads, scaled, lists, table, totals, *packets)
    sums = lax.all_to_all(sums, "head", 0, 0)
    kept = (heads, weights, slopes)
    narrow = ((C, 2 * F), bf16)
    blocks = (5, 7, 4, 6, 3, 2, 1)
    grads, acc, *parts = call(
        functools.partial(blocks_backward, blocks),
        [((2 * C, F), bf16), ((2 * C, F), f32)] + [narrow] * 7,
    )(att, sums, heads, scaled, weights, slopes, *(packets[b] for b in blocks))
    returned = [shifted(part, -DISTANCES[b - 1]) for b, part in zip(blocks, parts)]
    layer_out, grad_query, grad_gate, own = call(
        last_backward, [((C, F), bf16)] * 3 + [((C, 2 * F), f32)]
    )(grads, acc, *kept, packet, att, sums, gate_rows, cotangent, gain)
    grad_key, grad_value = call(total_kernel, [((C, F), bf16)] * 2)(own, *returned)
    return layer_out, grad_query, grad_key, grad_value, grad_gate


def solution(mesh):
    rows = P("seq", "head")
    return jax.shard_map(
        per_device,
        mesh=mesh,
        in_specs=(rows, rows, rows, rows, rows, P("seq"), P(), P("head", None), P("head")),
        out_specs=(rows, rows, rows, rows, rows),
        check_vma=False,
    )
```

```python
import functools

import jax
import jax.numpy as jnp
from jax import lax
from jax.experimental import pallas as pl
from jax.experimental.pallas import tpu as pltpu
from jax.sharding import PartitionSpec as P

norm_eps = 1e-05
C = 128
F = 128
DH = 64
DISTANCES = (1, 2, 4, 8, 16, 32, 64)
ROW = 32
PAD = 16
WIDE = 512.0
f32, bf16, i32 = jnp.float32, jnp.bfloat16, jnp.int32
VMEM = pl.BlockSpec(memory_space=pltpu.VMEM)
PARAMS = pltpu.CompilerParams(vmem_limit_bytes=40 * 1024 * 1024)


def iota(shape, dim):
    return lax.broadcasted_iota(i32, shape, dim)


def by_head(rows):
    left = iota(rows.shape, 1) < DH
    zero = jnp.zeros_like(rows)
    return jnp.concatenate([jnp.where(left, rows, zero), jnp.where(left, zero, rows)], axis=0)


def from_heads(both):
    left = iota((C, F), 1) < DH
    return jnp.where(left, both[:C], both[C:])


def dot(a, b, dims, precision=None):
    return lax.dot_general(a, b, (dims, ((), ())), preferred_element_type=f32, precision=precision)


NN, NT, TN = ((1,), (0,)), ((1,), (1,)), ((0,), (0,))


def pack_kernel(key_ref, value_ref, gaps_ref, out_ref, totals_ref, gaps_buf, sems):
    copies = [
        pltpu.make_async_copy(gaps_ref, gaps_buf, sems.at[0]),
        pltpu.make_async_copy(key_ref, out_ref.at[pl.ds(0, C), pl.ds(0, F)], sems.at[1]),
        pltpu.make_async_copy(value_ref, out_ref.at[pl.ds(0, C), pl.ds(F, F)], sems.at[2]),
    ]
    for copy in copies:
        copy.start()
    copies[0].wait()
    gaps = gaps_buf[...].astype(f32)
    total = jnp.sum(gaps, axis=1, keepdims=True)
    totals_ref[...] = jnp.broadcast_to(total.reshape(1, 1, 1), (ROW, 1, C))
    gaps = jnp.broadcast_to(gaps, (PAD, C)).astype(bf16)
    out_ref[C:, :F] = gaps
    out_ref[C:, F:] = gaps
    copies[1].wait()
    copies[2].wait()


def row_kernel(packet_ref, totals_ref, out_ref):
    out_ref[:C, :] = packet_ref[:C, :]
    totals = totals_ref[...].reshape(ROW, C)
    totals = jnp.where(iota((ROW, C), 0) == iota((ROW, C), 1), totals, 0.0)
    totals = jnp.sum(totals, axis=0, keepdims=True)
    high = jnp.floor(totals * 0.0625)
    low = totals - 16.0 * high
    line = iota((PAD, C), 0)
    gaps = packet_ref[C:, :F].astype(f32)
    out_ref[C:, :F] = jnp.where(line == 1, high, jnp.where(line == 2, low, gaps)).astype(bf16)
    out_ref[C:, F:] = packet_ref[C:, F:]


def prepare_kernel(query_ref, gate_ref, cot_ref, gain_ref, table_ref, lists_ref, *outs):
    heads_ref, scaled_ref, table_out_ref, lists_out_ref, row_ref = outs
    heads_ref[...] = by_head((query_ref[...].astype(f32) * 0.125).astype(bf16))
    scaled = cot_ref[...].astype(f32) * gate_ref[...].astype(f32) * gain_ref[...]
    scaled_ref[...] = scaled
    row_ref[...] = dot(jnp.ones((8, F), f32), scaled, NT, lax.Precision.HIGHEST)
    table_out_ref[...] = jnp.pad(table_ref[...], ((0, 0), (0, C - 16)))
    lists_out_ref[...] = lists_ref[...]


def forward_kernel(group_ref, heads_ref, scaled_ref, lists_ref, table_ref, row_ref, totals_ref, *refs):
    packets, (att_ref, sums_ref, weights_ref, slopes_ref) = refs[:8], refs[8:]
    group = group_ref[0]
    place = lax.rem(group, ROW)
    queries = heads_ref[...]
    gaps = jnp.concatenate([p[C : C + 1, :F] for p in packets], axis=0)
    upper = (iota((C, C), 0) <= iota((C, C), 1)).astype(bf16)
    key_times = dot(gaps, upper, NN)
    lower = (iota((C, C), 1) <= iota((C, C), 0)).astype(bf16)
    query_times = dot(lower, gaps, NT)[:, :1]
    own = totals_ref[...].reshape(ROW, C)
    own = jnp.where(iota((ROW, C), 0) == iota((ROW, C), 1), own, 0.0)
    totals = [jnp.sum(own, axis=0, keepdims=True)]
    for packet in packets[6:]:
        part = packet[C:, :F].astype(f32)
        totals.append(part[1:2, :] * 16.0 + part[2:3, :])
    lane = iota((8, C), 1)
    distance = jnp.left_shift(1, iota((8, C), 0)) >> 1
    between = jnp.zeros((8, C), f32)
    for r, total in enumerate(totals):
        back = place - lane + ROW * r
        inside = (back >= 1) & (back <= distance) & (lane < ROW)
        between = between + jnp.where(inside, total, 0.0)
    shifts = jnp.sum(between, axis=1, keepdims=True) - key_times
    listed = jnp.where(lane == group, lists_ref[...], 0)
    listed = jnp.sum(listed.astype(f32), axis=1, keepdims=True) >= 0.0
    listed = listed.astype(f32)
    tables = [jnp.broadcast_to(table_ref[h : h + 1, :], (C, C)) for h in range(2)]
    acc = jnp.zeros((2 * C, F), f32)
    for b, packet in enumerate(packets):
        scores = dot(queries, packet[:C, :F], NT)
        delta = (query_times + shifts[b : b + 1, :]).astype(i32)
        bucket = jnp.minimum(32 - lax.clz(delta), 15)
        bias = jnp.concatenate([jnp.take_along_axis(t, bucket, axis=1) for t in tables], axis=0)
        scores = scores + bias
        sig = 0.5 * jnp.tanh(0.5 * scores) + 0.5
        silu = scores * sig
        slope = sig + silu * (1.0 - sig)
        if b == 0:
            keep = (iota((C, C), 1) <= iota((C, C), 0)).astype(f32)
            keep = jnp.concatenate([keep, keep], axis=0)
        else:
            keep = listed[b - 1 : b, :]
        weights = (silu * keep).astype(bf16)
        weights_ref[:, b * C : (b + 1) * C] = weights
        slopes_ref[:, b * C : (b + 1) * C] = slope * keep
        acc = acc + dot(weights, packet[:C, F:], NN)
    att = from_heads(acc)
    att_ref[...] = att
    scaled = scaled_ref[...]
    terms = jnp.concatenate([att, att * att, scaled * att], axis=0)
    rows = dot(jnp.ones((8, F), f32), terms, NT, lax.Precision.HIGHEST)
    parts = [rows[0:1, r * C : (r + 1) * C] for r in range(3)]
    parts.insert(2, row_ref[0:1, :])
    for r in range(4):
        for x in range(4):
            sums_ref[x, r : r + 1, :] = parts[r]


def norm_terms(sums_ref, att_ref):
    sums = sums_ref[0] + sums_ref[1] + sums_ref[2] + sums_ref[3]
    sums = jnp.concatenate([sums, jnp.zeros((4, C), f32)], axis=0)
    cols = jnp.transpose(sums) * (1.0 / WIDE)
    mean, square, mean_scaled, mean_cross = (cols[:, r : r + 1] for r in range(4))
    inv_std = lax.rsqrt(square - mean * mean + norm_eps)
    mean_cross = (mean_cross - mean * mean_scaled) * inv_std
    return inv_std, (att_ref[...] - mean) * inv_std, mean_scaled, mean_cross


def block_grads(b, queries, grads, weights_ref, slopes_ref, packet, out_ref):
    at = slice(b * C, (b + 1) * C)
    grad_weights = dot(grads, packet[:C, F:], NT)
    grad_scores = (grad_weights * slopes_ref[:, at]).astype(bf16)
    out_ref[:, :F] = dot(grad_scores, queries, TN).astype(out_ref.dtype)
    out_ref[:, F:] = dot(weights_ref[:, at], grads, TN).astype(out_ref.dtype)
    return dot(grad_scores, packet[:C, :F], NN)


def blocks_backward(blocks, att_ref, sums_ref, heads_ref, scaled_ref, weights_ref, slopes_ref, *refs):
    n = len(blocks)
    packets, grads_ref, acc_ref, sent = refs[:n], refs[n], refs[n + 1], refs[n + 2 :]
    inv_std, centered, mean_scaled, mean_cross = norm_terms(sums_ref, att_ref)
    grads = inv_std * (scaled_ref[...] - mean_scaled - centered * mean_cross)
    grads = by_head(grads.astype(bf16))
    grads_ref[...] = grads
    queries = heads_ref[...]
    acc = jnp.zeros((2 * C, F), f32)
    for b, packet, out in zip(blocks, packets, sent):
        acc = acc + block_grads(b, queries, grads, weights_ref, slopes_ref, packet, out)
    acc_ref[...] = acc


def last_backward(
    grads_ref, before_ref, heads_ref, weights_ref, slopes_ref, packet, att_ref, sums_ref, gate_ref, cot_ref, gain_ref, *outs
):
    out_ref, dq_ref, dgate_ref, own_ref = outs
    acc = before_ref[...] + block_grads(
        0, heads_ref[...], grads_ref[...], weights_ref, slopes_ref, packet, own_ref
    )
    dq_ref[...] = (from_heads(acc) * 0.125).astype(bf16)
    centered = norm_terms(sums_ref, att_ref)[1]
    normed = centered * gain_ref[...]
    out_ref[...] = (normed * gate_ref[...].astype(f32)).astype(bf16)
    dgate_ref[...] = (cot_ref[...].astype(f32) * normed).astype(bf16)


def total_kernel(own_ref, *refs):
    parts, (dk_ref, dv_ref) = refs[:-2], refs[-2:]
    total = own_ref[...]
    for part in parts:
        total = total + part[...].astype(f32)
    dk_ref[...] = total[:, :F].astype(bf16)
    dv_ref[...] = total[:, F:].astype(bf16)


def call(kernel, outs, smem=0):
    def run(*args):
        specs = [pl.BlockSpec(memory_space=pltpu.SMEM)] * smem + [VMEM] * (len(args) - smem)
        return pl.pallas_call(
            kernel,
            out_shape=[jax.ShapeDtypeStruct(s, t) for s, t in outs],
            in_specs=specs,
            out_specs=[VMEM] * len(outs),
            compiler_params=PARAMS,
        )(*args)

    return run


def shifted(x, by):
    count = lax.axis_size("seq")
    return lax.ppermute(x, "seq", [(i, i + by) for i in range(count) if 0 <= i + by < count])


def per_device(
    query_rows,
    key_rows,
    value_rows,
    gate_rows,
    cotangent,
    event_gaps,
    block_lists,
    bias_table,
    norm_gain,
):
    count = lax.axis_size("seq")
    group = lax.axis_index("seq").astype(i32).reshape(1)
    gain = norm_gain.reshape(1, F)
    packet, totals = pl.pallas_call(
        pack_kernel,
        out_shape=[
            jax.ShapeDtypeStruct((C + PAD, 2 * F), bf16),
            jax.ShapeDtypeStruct((ROW, 1, C), f32),
        ],
        in_specs=[pl.BlockSpec(memory_space=pltpu.HBM)] * 3,
        out_specs=[VMEM] * 2,
        scratch_shapes=[pltpu.VMEM((1, C), i32), pltpu.SemaphoreType.DMA((3,))],
        compiler_params=pltpu.CompilerParams(vmem_limit_bytes=60 * 1024 * 1024),
    )(key_rows, value_rows, event_gaps.reshape(1, C))
    rows = [[y * ROW + k for k in range(ROW)] for y in range(count // ROW)]
    totals = lax.all_to_all(totals, "seq", 0, 0, axis_index_groups=rows)
    fetched = {d: shifted(packet, d) for d in (16, 8, 4, 2, 1)}
    (row_packet,) = call(row_kernel, [((C + PAD, 2 * F), bf16)])(packet, totals)
    fetched |= {d: shifted(row_packet, d) for d in (64, 32)}
    heads, scaled, table, lists, scaled_row = call(
        prepare_kernel,
        [((2 * C, F), bf16), ((C, F), f32), ((2, C), f32), ((8, C), i32), ((8, C), f32)],
    )(query_rows, gate_rows, cotangent, gain, bias_table, block_lists.T)
    packets = [packet] + [fetched[d] for d in DISTANCES]
    att, sums, weights, slopes = call(
        forward_kernel,
        [((C, F), f32), ((4, 4, C), f32), ((2 * C, 8 * C), bf16), ((2 * C, 8 * C), f32)],
        1,
    )(group, heads, scaled, lists, table, scaled_row, totals, *packets)
    sums = lax.all_to_all(sums, "head", 0, 0)
    kept = (heads, weights, slopes)
    narrow = ((C, 2 * F), bf16)
    blocks = (5, 7, 4, 6, 3, 2, 1)
    grads, acc, *parts = call(
        functools.partial(blocks_backward, blocks),
        [((2 * C, F), bf16), ((2 * C, F), f32)] + [narrow] * 7,
    )(att, sums, heads, scaled, weights, slopes, *(packets[b] for b in blocks))
    returned = [shifted(part, -DISTANCES[b - 1]) for b, part in zip(blocks, parts)]
    layer_out, grad_query, grad_gate, own = call(
        last_backward, [((C, F), bf16)] * 3 + [((C, 2 * F), f32)]
    )(grads, acc, *kept, packet, att, sums, gate_rows, cotangent, gain)
    grad_key, grad_value = call(total_kernel, [((C, F), bf16)] * 2)(own, *returned)
    return layer_out, grad_query, grad_key, grad_value, grad_gate


def solution(mesh):
    rows = P("seq", "head")
    return jax.shard_map(
        per_device,
        mesh=mesh,
        in_specs=(rows, rows, rows, rows, rows, P("seq"), P(), P("head", None), P("head")),
        out_specs=(rows, rows, rows, rows, rows),
        check_vma=False,
    )
```

```python
import functools

import jax
import jax.numpy as jnp
from jax import lax
from jax.experimental import pallas as pl
from jax.experimental.pallas import tpu as pltpu
from jax.sharding import PartitionSpec as P

norm_eps = 1e-05
C = 128
F = 128
DH = 64
DISTANCES = (1, 2, 4, 8, 16, 32, 64)
ROW = 32
PAD = 16
WIDE = 512.0
f32, bf16, i32 = jnp.float32, jnp.bfloat16, jnp.int32
VMEM = pl.BlockSpec(memory_space=pltpu.VMEM)
PARAMS = pltpu.CompilerParams(vmem_limit_bytes=40 * 1024 * 1024)


def iota(shape, dim):
    return lax.broadcasted_iota(i32, shape, dim)


def by_head(rows):
    left = iota(rows.shape, 1) < DH
    zero = jnp.zeros_like(rows)
    return jnp.concatenate([jnp.where(left, rows, zero), jnp.where(left, zero, rows)], axis=0)


def from_heads(both):
    left = iota((C, F), 1) < DH
    return jnp.where(left, both[:C], both[C:])


def dot(a, b, dims, precision=None):
    return lax.dot_general(a, b, (dims, ((), ())), preferred_element_type=f32, precision=precision)


NN, NT, TN = ((1,), (0,)), ((1,), (1,)), ((0,), (0,))


def pack_kernel(key_ref, value_ref, gaps_ref, out_ref, totals_ref, gaps_buf, sems):
    copies = [
        pltpu.make_async_copy(gaps_ref, gaps_buf, sems.at[0]),
        pltpu.make_async_copy(key_ref, out_ref.at[pl.ds(0, C), pl.ds(0, F)], sems.at[1]),
        pltpu.make_async_copy(value_ref, out_ref.at[pl.ds(0, C), pl.ds(F, F)], sems.at[2]),
    ]
    for copy in copies:
        copy.start()
    copies[0].wait()
    gaps = gaps_buf[...].astype(f32)
    total = jnp.sum(gaps, axis=1, keepdims=True)
    totals_ref[...] = jnp.broadcast_to(total.reshape(1, 1, 1), (ROW, 1, C))
    gaps = jnp.broadcast_to(gaps, (PAD, C)).astype(bf16)
    out_ref[C:, :F] = gaps
    out_ref[C:, F:] = gaps
    copies[1].wait()
    copies[2].wait()


def row_kernel(packet_ref, totals_ref, out_ref):
    out_ref[:C, :] = packet_ref[:C, :]
    totals = totals_ref[...].reshape(ROW, C)
    totals = jnp.where(iota((ROW, C), 0) == iota((ROW, C), 1), totals, 0.0)
    totals = jnp.sum(totals, axis=0, keepdims=True)
    high = jnp.floor(totals * 0.0625)
    low = totals - 16.0 * high
    line = iota((PAD, C), 0)
    gaps = packet_ref[C:, :F].astype(f32)
    out_ref[C:, :F] = jnp.where(line == 1, high, jnp.where(line == 2, low, gaps)).astype(bf16)
    out_ref[C:, F:] = packet_ref[C:, F:]


def prepare_kernel(query_ref, gate_ref, cot_ref, gain_ref, table_ref, lists_ref, *outs):
    heads_ref, scaled_ref, table_out_ref, lists_out_ref, row_ref = outs
    heads_ref[...] = by_head((query_ref[...].astype(f32) * 0.125).astype(bf16))
    scaled = cot_ref[...].astype(f32) * gate_ref[...].astype(f32) * gain_ref[...]
    scaled_ref[...] = scaled
    row_ref[...] = dot(jnp.ones((8, F), f32), scaled, NT, lax.Precision.HIGHEST)
    table_out_ref[...] = jnp.pad(table_ref[...], ((0, 0), (0, C - 16)))
    lists_out_ref[...] = lists_ref[...]


def forward_kernel(group_ref, heads_ref, scaled_ref, lists_ref, table_ref, row_ref, totals_ref, *refs):
    packets = refs[:6] + (refs[7], refs[6])
    att_ref, sums_ref, weights_ref, slopes_ref = refs[8:]
    group = group_ref[0]
    place = lax.rem(group, ROW)
    queries = heads_ref[...]
    gaps = jnp.concatenate([p[C : C + 1, :F] for p in packets], axis=0)
    upper = (iota((C, C), 0) <= iota((C, C), 1)).astype(bf16)
    key_times = dot(gaps, upper, NN)
    lower = (iota((C, C), 1) <= iota((C, C), 0)).astype(bf16)
    query_times = dot(lower, gaps, NT)[:, :1]
    own = totals_ref[...].reshape(ROW, C)
    own = jnp.where(iota((ROW, C), 0) == iota((ROW, C), 1), own, 0.0)
    totals = [jnp.sum(own, axis=0, keepdims=True)]
    for packet in packets[6:]:
        part = packet[C:, :F].astype(f32)
        totals.append(part[1:2, :] * 16.0 + part[2:3, :])
    lane = iota((8, C), 1)
    distance = jnp.left_shift(1, iota((8, C), 0)) >> 1
    between = jnp.zeros((8, C), f32)
    for r, total in enumerate(totals):
        back = place - lane + ROW * r
        inside = (back >= 1) & (back <= distance) & (lane < ROW)
        between = between + jnp.where(inside, total, 0.0)
    shifts = jnp.sum(between, axis=1, keepdims=True) - key_times
    listed = jnp.where(lane == group, lists_ref[...], 0)
    listed = jnp.sum(listed.astype(f32), axis=1, keepdims=True) >= 0.0
    listed = listed.astype(f32)
    tables = [jnp.broadcast_to(table_ref[h : h + 1, :], (C, C)) for h in range(2)]
    acc = jnp.zeros((2 * C, F), f32)
    for b, packet in enumerate(packets):
        scores = dot(queries, packet[:C, :F], NT)
        delta = (query_times + shifts[b : b + 1, :]).astype(i32)
        bucket = jnp.minimum(32 - lax.clz(delta), 15)
        bias = jnp.concatenate([jnp.take_along_axis(t, bucket, axis=1) for t in tables], axis=0)
        scores = scores + bias
        sig = 0.5 * jnp.tanh(0.5 * scores) + 0.5
        silu = scores * sig
        slope = sig + silu * (1.0 - sig)
        if b == 0:
            keep = (iota((C, C), 1) <= iota((C, C), 0)).astype(f32)
            keep = jnp.concatenate([keep, keep], axis=0)
        else:
            keep = listed[b - 1 : b, :]
        weights = (silu * keep).astype(bf16)
        weights_ref[:, b * C : (b + 1) * C] = weights
        slopes_ref[:, b * C : (b + 1) * C] = slope * keep
        acc = acc + dot(weights, packet[:C, F:], NN)
    att = from_heads(acc)
    att_ref[...] = att
    scaled = scaled_ref[...]
    terms = jnp.concatenate([att, att * att, scaled * att], axis=0)
    rows = dot(jnp.ones((8, F), f32), terms, NT, lax.Precision.HIGHEST)
    parts = [rows[0:1, r * C : (r + 1) * C] for r in range(3)]
    parts.insert(2, row_ref[0:1, :])
    for r in range(4):
        for x in range(4):
            sums_ref[x, r : r + 1, :] = parts[r]


def norm_terms(sums_ref, att_ref):
    sums = sums_ref[0] + sums_ref[1] + sums_ref[2] + sums_ref[3]
    sums = jnp.concatenate([sums, jnp.zeros((4, C), f32)], axis=0)
    cols = jnp.transpose(sums) * (1.0 / WIDE)
    mean, square, mean_scaled, mean_cross = (cols[:, r : r + 1] for r in range(4))
    inv_std = lax.rsqrt(square - mean * mean + norm_eps)
    mean_cross = (mean_cross - mean * mean_scaled) * inv_std
    return inv_std, (att_ref[...] - mean) * inv_std, mean_scaled, mean_cross


def block_grads(b, queries, grads, weights_ref, slopes_ref, packet, out_ref):
    at = slice(b * C, (b + 1) * C)
    grad_weights = dot(grads, packet[:C, F:], NT)
    grad_scores = (grad_weights * slopes_ref[:, at]).astype(bf16)
    out_ref[:, :F] = dot(grad_scores, queries, TN).astype(out_ref.dtype)
    out_ref[:, F:] = dot(weights_ref[:, at], grads, TN).astype(out_ref.dtype)
    return dot(grad_scores, packet[:C, :F], NN)


def blocks_backward(blocks, att_ref, sums_ref, heads_ref, scaled_ref, weights_ref, slopes_ref, *refs):
    n = len(blocks)
    packets, grads_ref, acc_ref, sent = refs[:n], refs[n], refs[n + 1], refs[n + 2 :]
    inv_std, centered, mean_scaled, mean_cross = norm_terms(sums_ref, att_ref)
    grads = inv_std * (scaled_ref[...] - mean_scaled - centered * mean_cross)
    grads = by_head(grads.astype(bf16))
    grads_ref[...] = grads
    queries = heads_ref[...]
    acc = jnp.zeros((2 * C, F), f32)
    for b, packet, out in zip(blocks, packets, sent):
        acc = acc + block_grads(b, queries, grads, weights_ref, slopes_ref, packet, out)
    acc_ref[...] = acc


def last_backward(
    grads_ref, before_ref, heads_ref, weights_ref, slopes_ref, packet, att_ref, sums_ref, gate_ref, cot_ref, gain_ref, *outs
):
    out_ref, dq_ref, dgate_ref, own_ref = outs
    acc = before_ref[...] + block_grads(
        0, heads_ref[...], grads_ref[...], weights_ref, slopes_ref, packet, own_ref
    )
    dq_ref[...] = (from_heads(acc) * 0.125).astype(bf16)
    centered = norm_terms(sums_ref, att_ref)[1]
    normed = centered * gain_ref[...]
    out_ref[...] = (normed * gate_ref[...].astype(f32)).astype(bf16)
    dgate_ref[...] = (cot_ref[...].astype(f32) * normed).astype(bf16)


def total_kernel(own_ref, *refs):
    parts, (dk_ref, dv_ref) = refs[:-2], refs[-2:]
    total = own_ref[...]
    for part in parts:
        total = total + part[...].astype(f32)
    dk_ref[...] = total[:, :F].astype(bf16)
    dv_ref[...] = total[:, F:].astype(bf16)


def call(kernel, outs, smem=0):
    def run(*args):
        specs = [pl.BlockSpec(memory_space=pltpu.SMEM)] * smem + [VMEM] * (len(args) - smem)
        return pl.pallas_call(
            kernel,
            out_shape=[jax.ShapeDtypeStruct(s, t) for s, t in outs],
            in_specs=specs,
            out_specs=[VMEM] * len(outs),
            compiler_params=PARAMS,
        )(*args)

    return run


def shifted(x, by):
    count = lax.axis_size("seq")
    return lax.ppermute(x, "seq", [(i, i + by) for i in range(count) if 0 <= i + by < count])


def per_device(
    query_rows,
    key_rows,
    value_rows,
    gate_rows,
    cotangent,
    event_gaps,
    block_lists,
    bias_table,
    norm_gain,
):
    count = lax.axis_size("seq")
    group = lax.axis_index("seq").astype(i32).reshape(1)
    gain = norm_gain.reshape(1, F)
    packet, totals = pl.pallas_call(
        pack_kernel,
        out_shape=[
            jax.ShapeDtypeStruct((C + PAD, 2 * F), bf16),
            jax.ShapeDtypeStruct((ROW, 1, C), f32),
        ],
        in_specs=[pl.BlockSpec(memory_space=pltpu.HBM)] * 3,
        out_specs=[VMEM] * 2,
        scratch_shapes=[pltpu.VMEM((1, C), i32), pltpu.SemaphoreType.DMA((3,))],
        compiler_params=pltpu.CompilerParams(vmem_limit_bytes=60 * 1024 * 1024),
    )(key_rows, value_rows, event_gaps.reshape(1, C))
    rows = [[y * ROW + k for k in range(ROW)] for y in range(count // ROW)]
    totals = lax.all_to_all(totals, "seq", 0, 0, axis_index_groups=rows)
    fetched = {d: shifted(packet, d) for d in (16, 8, 4, 2, 1)}
    (row_packet,) = call(row_kernel, [((C + PAD, 2 * F), bf16)])(packet, totals)
    fetched |= {d: shifted(row_packet, d) for d in (64, 32)}
    heads, scaled, table, lists, scaled_row = call(
        prepare_kernel,
        [((2 * C, F), bf16), ((C, F), f32), ((2, C), f32), ((8, C), i32), ((8, C), f32)],
    )(query_rows, gate_rows, cotangent, gain, bias_table, block_lists.T)
    packets = [packet] + [fetched[d] for d in DISTANCES]
    att, sums, weights, slopes = call(
        forward_kernel,
        [((C, F), f32), ((4, 4, C), f32), ((2 * C, 8 * C), bf16), ((2 * C, 8 * C), f32)],
        1,
    )(group, heads, scaled, lists, table, scaled_row, totals, *packets[:6], packets[7], packets[6])
    sums = lax.all_to_all(sums, "head", 0, 0)
    kept = (heads, weights, slopes)
    narrow = ((C, 2 * F), bf16)
    blocks = (5, 7, 4, 6, 3, 2, 1)
    grads, acc, *parts = call(
        functools.partial(blocks_backward, blocks),
        [((2 * C, F), bf16), ((2 * C, F), f32)] + [narrow] * 7,
    )(att, sums, heads, scaled, weights, slopes, *(packets[b] for b in blocks))
    returned = [shifted(part, -DISTANCES[b - 1]) for b, part in zip(blocks, parts)]
    layer_out, grad_query, grad_gate, own = call(
        last_backward, [((C, F), bf16)] * 3 + [((C, 2 * F), f32)]
    )(grads, acc, *kept, packet, att, sums, gate_rows, cotangent, gain)
    grad_key, grad_value = call(total_kernel, [((C, F), bf16)] * 2)(own, *returned)
    return layer_out, grad_query, grad_key, grad_value, grad_gate


def solution(mesh):
    rows = P("seq", "head")
    return jax.shard_map(
        per_device,
        mesh=mesh,
        in_specs=(rows, rows, rows, rows, rows, P("seq"), P(), P("head", None), P("head")),
        out_specs=(rows, rows, rows, rows, rows),
        check_vma=False,
    )
```
